32 devices in a mesh: segaz: 8 (over y, x, core), rad: 4 (over z).
Axes of the slice: x: 2, y: 2, z: 4, core: 2. Of those that a mesh axis runs over, the one named last changes fastest.
Arguments:
- state: float32 [5, 2048, 1024], P(None, 'segaz', 'rad'), may hold values from -6 to 6
- kappa: float32 [2048, 1024], P('segaz', 'rad'), may hold values from 0.1 to 1
- drop_src: float32 [5, 1048576], P(None, ('segaz', 'rad')), may hold values from -48 to 48
- drop_cell: int32 [1048576], P(('segaz', 'rad')), may hold values from 0 to 65535
- drop_count: int32 [32, 8], P(('segaz', 'rad')), may hold values from 1 to 5120, 32768 in all within a row
- part_map: int32 [8], replicated, may hold values from 0 to 7, as said below
- match_block: int32 [8], replicated, may hold values from 0 to 7, as said below
Outputs:
- new_state: float32 [5, 2048, 1024], P(None, 'segaz', 'rad')
The draws below stay inside these ranges and needn't reach their ends.
Inputs may be any that keep to these rules, and one draw needn't show every extreme that they name: Each row of drop_count sums to 32768; a partition's droplet rows are grouped by destination in increasing segaz index: its first drop_count[p, 0] rows go to index 0, the next drop_count[p, 1] to index 1, and so on. Every row reaches the maximum. `part_map`: A permutation of the block ids. match_block[match_block[b]] = b and match_block[b] != b for every block b.
All inputs are finite; a program needn't handle non-finite values.
Results may differ from the reference program's by a relative error of at most 0.0003.
Values sent between devices are 32-bit elements; how exact they have to be, the bound alone decides.
No kernel may reach another device: no remote copies, remote signals or barrier semaphores. Data moves between devices by JAX's collectives and lax.ppermute only.
A program may use at most 128 MiB of HBM per device.

```python
import math
import jax
import jax.numpy as jnp
import numpy as np
from jax import lax

NV = 5
CA = 256
CR = 256
DROP_DEV = 32768
FW = 4
JL = 4
NA = 2048
NR = 1024
NPART = 32
NDROP = 1048576
N_SEGAZ = 8
N_RAD = 4


def block_order(key):
    return jax.random.permutation(jax.random.fold_in(key, 11), N_SEGAZ).astype(jnp.int32)


def draw_part_map(key, part):
    order = block_order(key)
    return order


def draw_match_block(key, part):
    order = block_order(key)
    key = jax.random.fold_in(key, 7)
    first_key, rest_key = jax.random.split(key)
    start = jax.random.randint(first_key, (), 0, N_SEGAZ).astype(jnp.int32)
    rest = ((start + 2 + jnp.arange(N_SEGAZ - 2, dtype=jnp.int32)) % N_SEGAZ).astype(jnp.int32)
    rest = rest[jax.random.permutation(rest_key, N_SEGAZ - 2)]
    listing = jnp.concatenate([jnp.stack([start, (start + 1) % N_SEGAZ]), rest]).astype(jnp.int32)
    evens = listing[0::2]
    odds = listing[1::2]
    mate = jnp.zeros((N_SEGAZ,), jnp.int32).at[evens].set(odds).at[odds].set(evens)
    return jnp.zeros((N_SEGAZ,), jnp.int32).at[order].set(order[mate])


def touch_ends(result, rng, low, high):
    longest = result.shape.index(max(result.shape))
    spots = []
    for shift in (0, 1):
        where = [jax.random.randint(jax.random.fold_in(rng, axis), (), 0, length) for axis, length in enumerate(result.shape)]
        where[longest] = (where[longest] + shift) % result.shape[longest]
        spots.append(tuple(where))
    return result.at[spots[0]].set(low).at[spots[1]].set(high)


def block_levels(key, dims, pieces, low, high):
    loudness, own = 1.0, jax.random.fold_in(key, 6)
    for dim, parts in pieces:
        heights = jnp.exp(jax.random.uniform(jax.random.fold_in(own, dim), (parts,), jnp.float32, low / len(pieces), high / len(pieces)))
        loudness = loudness * jnp.repeat(heights, dims[dim] // parts).reshape([-1 if axis == dim else 1 for axis in range(len(dims))])
    return loudness


def length_profile(number_of, total, limit, slope):
    portions = [(1 << 20) // math.isqrt(standing ** slope) + 1 for standing in range(2, number_of + 1)]
    spare, holding = total - limit - (number_of - 1), [1] * (number_of - 1)
    while spare > 0:
        free = [i for i in range(number_of - 1) if holding[i] < limit]
        pool, remaining = sum([portions[i] for i in free]), spare
        for i in free:
            more = min(limit - holding[i], max(1, remaining * portions[i] // pool), spare)
            holding[i] = holding[i] + more
            spare = spare - more
    return np.array([limit] + holding)


def uneven_parts(stream_key, count, total, bound, skew):
    if count == 2:
        one = jax.random.randint(stream_key, (), max(1, total - bound), min(bound, total - 1) + 1)
        return jnp.stack([one, total - one])
    tallies = jnp.asarray(length_profile(count, total, bound, skew), jnp.int32)
    pairs = (count - 1) // 2
    donor, sink = tallies[1:1 + 2 * pairs:2], tallies[2:2 + 2 * pairs:2]
    margin = jnp.minimum(donor - 1, bound - sink)
    passed = jax.random.randint(jax.random.fold_in(stream_key, 1), (pairs,), 0, 1 << 20) % (margin + 1)
    tallies = tallies.at[1:1 + 2 * pairs:2].set(donor - passed).at[2:2 + 2 * pairs:2].set(sink + passed)
    return tallies[jax.random.permutation(jax.random.fold_in(stream_key, 2), count)]


def noise(rng, shape, spread, bound, cuts=(), kind=jnp.bfloat16):
    drawn = spread * jax.random.normal(rng, shape, jnp.float32)
    if cuts:
        drawn = drawn * block_levels(rng, shape, cuts, -0.22, 0.18)
    return jnp.clip(drawn, -bound, bound).astype(kind)


def setup_inputs(seed: int = 0) -> dict:
    seeds = jax.random.split(jax.random.key(seed), 8)
    state = noise(seeds[0], (NV, NA, NR), 1.0, 6.0, ((1, 8), (2, 4)), jnp.float32)
    kappa = jnp.clip(jnp.exp(math.log(1.0) - 2.3025851 * jax.random.uniform(seeds[1], (NA, NR), jnp.float32) ** block_levels(seeds[1], (NA, NR), ((0, 8), (1, 4)), -0.2, 0.2)), 0.1, 1.0)
    drop_src = noise(seeds[2], (NV, NDROP), 8.0, 48.0, ((1, 32),), jnp.float32)
    drop_cell = touch_ends(jax.random.randint(seeds[3], (NDROP,), 0, CA * CR), jax.random.fold_in(seeds[3], 1), 0, (CA * CR) - 1).astype(jnp.int32)
    drop_count = jax.vmap(lambda own: uneven_parts(own, N_SEGAZ, DROP_DEV, 5 * DROP_DEV // (4 * N_SEGAZ), 2))(jax.random.split(seeds[4], NPART)).reshape((NPART, N_SEGAZ)).astype(jnp.int32)
    part_map = draw_part_map(jax.random.fold_in(seeds[7], 71), 0)
    match_block = draw_match_block(jax.random.fold_in(seeds[7], 71), 0)
    return dict(state=state, kappa=kappa, drop_src=drop_src, drop_cell=drop_cell, drop_count=drop_count, part_map=part_map, match_block=match_block)


time_step = 0.25
layer_weights = (1.0, 0.6, 0.35, 0.2)


def filter_weights(half_width):
    offsets = jnp.arange(-half_width, half_width + 1).astype(jnp.float32)
    bell_curve = jnp.exp(-offsets * offsets / 8.0)
    return bell_curve / jnp.sum(bell_curve)


def smooth_axis(padded, half_width, axis_dim, length):
    weights = filter_weights(half_width)
    summed = weights[0] * lax.slice_in_dim(padded, 0, length, axis=axis_dim)
    for tap_index in range(1, 2 * half_width + 1):
        summed = summed + weights[tap_index] * lax.slice_in_dim(padded, tap_index, tap_index + length, axis=axis_dim)
    return summed


def laplace_nine(padded):
    centre = padded[:, 1:-1, 1:-1]
    edge_sum = padded[:, 2:, 1:-1] + padded[:, :-2, 1:-1] + padded[:, 1:-1, 2:] + padded[:, 1:-1, :-2]
    corners = padded[:, 2:, 2:] + padded[:, 2:, :-2] + padded[:, :-2, 2:] + padded[:, :-2, :-2]
    return (4.0 * edge_sum + corners - 20.0 * centre) / 6.0


def find_group(group_ends, local_rows):
    return jnp.searchsorted(group_ends, local_rows, side="right").astype(jnp.int32)


def reference(state, kappa, drop_src, drop_cell, drop_count, part_map, match_block):
    components, azim_total, radial_total = state.shape
    part_count = drop_count.shape[0]
    group_ends = jnp.cumsum(drop_count, axis=1).astype(jnp.int32)
    local_rows = jnp.arange(DROP_DEV).astype(jnp.int32)
    dest_part = jax.vmap(find_group, in_axes=(0, None))(group_ends, local_rows)
    radial_block = (jnp.arange(part_count).astype(jnp.int32) % N_RAD)[:, None]
    cell_ids = drop_cell.reshape(part_count, DROP_DEV)
    azim_index = dest_part * CA + cell_ids // CR
    radial_index = radial_block * CR + cell_ids % CR
    flat_index = (azim_index * radial_total + radial_index).reshape(-1).astype(jnp.int32)
    source = jnp.zeros((components, azim_total * radial_total), jnp.float32).at[:, flat_index].add(drop_src)
    source = source.reshape(components, azim_total, radial_total)
    wide_azim = jnp.pad(source, ((0, 0), (FW, FW), (0, 0)))
    smoothed = smooth_axis(wide_azim, FW, 1, azim_total)
    wide_radial = jnp.pad(smoothed, ((0, 0), (0, 0), (FW, FW)))
    filtered = smooth_axis(wide_radial, FW, 2, radial_total)
    diffusion = kappa[None] * laplace_nine(jnp.pad(state, ((0, 0), (1, 1), (1, 1))))
    indices = jnp.arange(N_SEGAZ).astype(jnp.int32)
    target = match_block[part_map]
    partner = jnp.sum(jnp.where(part_map[None, :] == target[:, None], indices[None, :], 0), axis=1).astype(jnp.int32)
    by_block = state.reshape(components, N_SEGAZ, CA, radial_total)
    face_rows = by_block[:, :, :JL, :]
    partner_face = face_rows[:, partner]
    weights = jnp.array(layer_weights, jnp.float32)[:JL]
    coupling = weights[None, None, :, None] * (partner_face - face_rows)
    junction = jnp.zeros_like(by_block).at[:, :, :JL, :].set(coupling).reshape(components, azim_total, radial_total)
    return state + time_step * (diffusion + junction + filtered)
```

```python
import functools

import jax
import jax.numpy as jnp
from jax import lax
from jax.experimental import pallas as pl
from jax.experimental.pallas import tpu as pltpu
from jax.sharding import PartitionSpec as P

FW = 4
JL = 4
LANES = 128

time_step = 0.25
layer_weights = (1.0, 0.6, 0.35, 0.2)


def extended(cells, sides, width):
    for axis, dim in sides:
        count = lax.axis_size(axis)
        ends = count - 1
        head = lax.slice_in_dim(cells, 0, width, axis=dim)
        tail = lax.slice_in_dim(cells, cells.shape[dim] - width, cells.shape[dim], axis=dim)
        cells = jnp.concatenate(
            [
                lax.ppermute(tail, axis, [(i, (i + 1) % count) for i in range(ends)]),
                cells,
                lax.ppermute(head, axis, [((i + 1) % count, i) for i in range(ends)]),
            ],
            axis=dim,
        )
    return cells


def filter_weights(half_width):
    offsets = jnp.arange(-half_width, half_width + 1).astype(jnp.float32)
    bell_curve = jnp.exp(-offsets * offsets / 8.0)
    return bell_curve / jnp.sum(bell_curve)


def smooth_axis(padded, half_width, axis_dim, length):
    weights = filter_weights(half_width)
    summed = weights[0] * lax.slice_in_dim(padded, 0, length, axis=axis_dim)
    for tap_index in range(1, 2 * half_width + 1):
        summed = summed + weights[tap_index] * lax.slice_in_dim(
            padded, tap_index, tap_index + length, axis=axis_dim
        )
    return summed


def laplace_nine(padded):
    centre = padded[:, 1:-1, 1:-1]
    edge_sum = (
        padded[:, 2:, 1:-1] + padded[:, :-2, 1:-1] + padded[:, 1:-1, 2:] + padded[:, 1:-1, :-2]
    )
    corners = padded[:, 2:, 2:] + padded[:, 2:, :-2] + padded[:, :-2, 2:] + padded[:, :-2, :-2]
    return (4.0 * edge_sum + corners - 20.0 * centre) / 6.0


def pack_kernel(cap_tiles, base, count_ref, src_ref, cell_ref, state_ref, out_ref):
    seg_count = out_ref.shape[0]
    components = src_ref.shape[0]
    fields = components + 1
    tile_count = cell_ref.shape[0]
    lane = lax.broadcasted_iota(jnp.int32, (8, LANES), 1)
    sub = lax.broadcasted_iota(jnp.int32, (8, LANES), 0)

    def slot(g, begin):
        count = count_ref[0, g]
        first = begin // LANES
        shift = begin % LANES
        turn = (LANES - shift) % LANES

        def rolled(i):
            t = jnp.minimum(first + i, tile_count - 1)
            src = src_ref[:, pl.ds(pl.multiple_of(t * LANES, LANES), LANES)]
            cell = cell_ref[pl.ds(t, 1), :].astype(jnp.float32)
            both = jnp.concatenate([src, cell, jnp.zeros((8 - fields, LANES), jnp.float32)], axis=0)
            return pltpu.roll(both, turn, 1)

        for v in range(components):
            for half in range(2):
                out_ref[g, 8 * v + 4 * half : 8 * v + 4 * half + JL, :] = state_ref[
                    v, 0:JL, half * LANES : (half + 1) * LANES
                ]
        head = rolled(0)
        for i in range(cap_tiles):
            tail = rolled(i + 1)
            rows = jnp.where(lane < LANES - shift, head, tail)
            dead = (sub == components) & (lane >= count - i * LANES)
            rows = jnp.where(dead, -1.0 - count.astype(jnp.float32), rows)
            out_ref[g, base + fields * i : base + fields * (i + 1), :] = rows[:fields]
            head = tail
        return begin + count

    lax.fori_loop(0, seg_count, slot, jnp.int32(0))


def deposit_kernel(cap_tiles, base, step, got_ref, out_ref):
    seg_count = got_ref.shape[0]
    components = out_ref.shape[0]
    azim, radial = out_ref.shape[1:]
    fields = components + 1
    width = step * LANES
    end = base + fields * cap_tiles
    lane = lax.broadcasted_iota(jnp.int32, (1, LANES), 1)
    cells = lax.broadcasted_iota(jnp.int32, (azim, width), 0).astype(jnp.float32).astype(jnp.bfloat16)
    out_ref[...] = jnp.zeros(out_ref.shape, jnp.float32)

    def slot(s, carry):
        tail = got_ref[s, end - 1 : end, :]
        mark = jnp.sum(jnp.where(lane == LANES - 1, tail, 0.0)).astype(jnp.int32)
        count = jnp.where(mark >= 0, cap_tiles * LANES, -1 - mark)

        def chunk(j, carry):
            rows = got_ref[s, pl.ds(pl.multiple_of(base + fields * step * j, 8), fields * step), :]

            def field(k):
                return jnp.concatenate(
                    [rows[fields * q + k : fields * q + k + 1] for q in range(step)], axis=1
                )

            ids = field(components)
            a = jnp.floor(ids * (1.0 / radial))
            b = (ids - radial * a).astype(jnp.bfloat16)
            in_b = jnp.where(cells == b, jnp.bfloat16(1), jnp.bfloat16(0))
            in_a = cells == a.astype(jnp.bfloat16)
            right = jnp.concatenate([in_b, in_b], axis=1)
            for v in range(components):
                values = field(v)
                high = values.astype(jnp.bfloat16)
                low = (values - high.astype(jnp.float32)).astype(jnp.bfloat16)
                left = jnp.concatenate(
                    [jnp.where(in_a, high, jnp.bfloat16(0)), jnp.where(in_a, low, jnp.bfloat16(0))],
                    axis=1,
                )
                out_ref[v] += lax.dot_general(
                    left, right, (((1,), (1,)), ((), ())), preferred_element_type=jnp.float32
                )
            return carry

        return lax.fori_loop(0, (count + width - 1) // width, chunk, carry)

    lax.fori_loop(0, seg_count, slot, 0)


def local(state, kappa, drop_src, drop_cell, drop_count, part_map, match_block):
    components, azim_cells, radial_cells = state.shape
    row_count = drop_src.shape[1]
    seg_count = lax.axis_size("segaz")
    capacity = 5 * row_count // (4 * seg_count)
    cap_tiles = capacity // LANES
    step = 4 if cap_tiles % 4 == 0 else 2
    base = 8 * components
    fields = components + 1
    slot_rows = -(-(base + fields * cap_tiles) // 8) * 8
    own_index = lax.axis_index("segaz")
    indices = jnp.arange(seg_count, dtype=jnp.int32)
    vmem = pl.BlockSpec(memory_space=pltpu.VMEM)
    smem = pl.BlockSpec(memory_space=pltpu.SMEM)
    sends = pl.pallas_call(
        functools.partial(pack_kernel, cap_tiles, base),
        out_shape=jax.ShapeDtypeStruct((seg_count, slot_rows, LANES), jnp.float32),
        in_specs=[smem, vmem, vmem, vmem],
        out_specs=vmem,
        compiler_params=pltpu.CompilerParams(vmem_limit_bytes=48 << 20),
    )(drop_count, drop_src, drop_cell.reshape(-1, LANES), state)
    got = lax.all_to_all(sends, "segaz", split_axis=0, concat_axis=0, tiled=True)
    source = pl.pallas_call(
        functools.partial(deposit_kernel, cap_tiles, base, step),
        out_shape=jax.ShapeDtypeStruct(state.shape, jnp.float32),
        in_specs=[vmem],
        out_specs=vmem,
        compiler_params=pltpu.CompilerParams(vmem_limit_bytes=48 << 20),
    )(got)

    padded = extended(state, (("segaz", 1), ("rad", 2)), 1)
    diffusion = kappa[None] * laplace_nine(padded)
    my_block = jnp.sum(jnp.where(indices == own_index, part_map, 0))
    target = jnp.sum(jnp.where(indices == my_block, match_block, 0))
    partner = jnp.sum(jnp.where(part_map == target, indices, 0))
    face_rows = state[:, :JL, :]
    partner_face = lax.dynamic_index_in_dim(got, partner, 0, keepdims=False)[:base]
    partner_face = partner_face.reshape(components, 2, JL, LANES).transpose(0, 2, 1, 3).reshape(face_rows.shape)
    weights = jnp.array(layer_weights, jnp.float32)
    coupling = weights[None, :, None] * (partner_face - face_rows)
    junction = jnp.concatenate(
        [coupling, jnp.zeros((components, azim_cells - JL, radial_cells), jnp.float32)], axis=1
    )
    wide_azim = extended(source, (("segaz", 1),), FW)
    smoothed = smooth_axis(wide_azim, FW, 1, azim_cells)
    wide_radial = extended(smoothed, (("rad", 2),), FW)
    filtered = smooth_axis(wide_radial, FW, 2, radial_cells)
    return state + time_step * (diffusion + junction + filtered)


def solution(mesh):
    return jax.shard_map(
        local,
        mesh=mesh,
        in_specs=(
            P(None, "segaz", "rad"),
            P("segaz", "rad"),
            P(None, ("segaz", "rad")),
            P(("segaz", "rad")),
            P(("segaz", "rad"), None),
            P(),
            P(),
        ),
        out_specs=P(None, "segaz", "rad"),
        check_vma=False,
    )
```

```python
import functools

import jax
import jax.numpy as jnp
from jax import lax
from jax.experimental import pallas as pl
from jax.experimental.pallas import tpu as pltpu
from jax.sharding import PartitionSpec as P

FW = 4
JL = 4
LANES = 128
WINDOW = 64
ROUNDS = 2
UNROLL = 8
WIDE = False
STEP = 4

time_step = 0.25
layer_weights = (1.0, 0.6, 0.35, 0.2)


def extended(cells, sides, width):
    for axis, dim in sides:
        count = lax.axis_size(axis)
        ends = count - 1
        head = lax.slice_in_dim(cells, 0, width, axis=dim)
        tail = lax.slice_in_dim(cells, cells.shape[dim] - width, cells.shape[dim], axis=dim)
        cells = jnp.concatenate(
            [
                lax.ppermute(tail, axis, [(i, (i + 1) % count) for i in range(ends)]),
                cells,
                lax.ppermute(head, axis, [((i + 1) % count, i) for i in range(ends)]),
            ],
            axis=dim,
        )
    return cells


def filter_weights(half_width):
    offsets = jnp.arange(-half_width, half_width + 1).astype(jnp.float32)
    bell_curve = jnp.exp(-offsets * offsets / 8.0)
    return bell_curve / jnp.sum(bell_curve)


def smooth_axis(padded, half_width, axis_dim, length):
    weights = filter_weights(half_width)
    summed = weights[0] * lax.slice_in_dim(padded, 0, length, axis=axis_dim)
    for tap_index in range(1, 2 * half_width + 1):
        summed = summed + weights[tap_index] * lax.slice_in_dim(
            padded, tap_index, tap_index + length, axis=axis_dim
        )
    return summed


def laplace_nine(padded):
    centre = padded[:, 1:-1, 1:-1]
    edge_sum = (
        padded[:, 2:, 1:-1] + padded[:, :-2, 1:-1] + padded[:, 1:-1, 2:] + padded[:, 1:-1, :-2]
    )
    corners = padded[:, 2:, 2:] + padded[:, 2:, :-2] + padded[:, :-2, 2:] + padded[:, :-2, :-2]
    return (4.0 * edge_sum + corners - 20.0 * centre) / 6.0


def comparators(count):
    size = 1 << (count - 1).bit_length()
    pairs = []
    p = 1
    while p < size:
        k = p
        while k >= 1:
            for j in range(k % p, size - k, 2 * k):
                for i in range(min(k, size - j - k)):
                    if (i + j) // (2 * p) == (i + j + k) // (2 * p) and i + j + k < count:
                        pairs.append((i + j, i + j + k))
            k //= 2
        p *= 2
    return pairs


def sort_rows(tiles):
    pairs = comparators(len(tiles))
    for low, high in pairs:
        swap = tiles[high][-1] < tiles[low][-1]
        first = [jnp.where(swap, y, x) for x, y in zip(tiles[low], tiles[high])]
        second = [jnp.where(swap, x, y) for x, y in zip(tiles[low], tiles[high])]
        tiles[low], tiles[high] = first, second
    return tiles


def pack_kernel(cap_tiles, step, base, count_ref, src_ref, cell_ref, state_ref, out_ref, held_ref):
    components = src_ref.shape[0]
    fields = components + 1
    tile_count = cell_ref.shape[0]
    radial = state_ref.shape[2]
    azim = state_ref.shape[1]
    slot_rows = base + 8 + -(-fields * cap_tiles // 8) * 8
    seg_count = out_ref.shape[0] // slot_rows
    lane = lax.broadcasted_iota(jnp.int32, (8, LANES), 1)
    sub = lax.broadcasted_iota(jnp.int32, (8, LANES), 0)
    none = float(azim * radial)

    def slot(g, begin):
        count = count_ref[0, g]
        first = begin // LANES
        shift = begin % LANES
        turn = (LANES - shift) % LANES

        def rolled(i):
            t = jnp.minimum(first + i, tile_count - 1)
            src = src_ref[:, pl.ds(pl.multiple_of(t * LANES, LANES), LANES)]
            cell = cell_ref[pl.ds(t, 1), :].astype(jnp.float32)
            both = jnp.concatenate([src, cell, jnp.zeros((8 - fields, LANES), jnp.float32)], axis=0)
            return pltpu.roll(both, turn, 1)

        row = g * slot_rows
        for v in range(components):
            for half in range(2):
                out_ref[pl.ds(row + 8 * v + 4 * half, JL), :] = state_ref[
                    v, 0:JL, half * LANES : (half + 1) * LANES
                ]
        head = rolled(0)
        for i in range(cap_tiles):
            tail = rolled(i + 1)
            rows = jnp.where(lane < LANES - shift, head, tail)
            dead = (sub == components) & (lane >= count - i * LANES)
            rows = jnp.where(dead, none, rows)
            held_ref[g // 8, i, pl.ds(g % 8, 8, stride=8), :] = rows
            head = tail
        return begin + count

    lax.fori_loop(0, seg_count, slot, jnp.int32(0))

    def group(h, carry):
        tiles = [
            [held_ref[h, i, 8 * f : 8 * f + 8, :] for f in range(fields)] for i in range(cap_tiles)
        ]
        tiles = sort_rows(tiles)
        for again in range(ROUNDS - 1):
            tiles = [[pltpu.roll(x, (37 * i) % LANES, 1) for x in tiles[i]] for i in range(cap_tiles)]
            tiles = sort_rows(tiles)
        row = h * 8 * slot_rows
        bounds = jnp.zeros((8, LANES), jnp.float32)
        for j in range(cap_tiles // step):
            keys = [tiles[i][-1] for i in range(step * j, step * j + step)]
            least = jnp.min(keys[0], axis=1, keepdims=True)
            most = keys[0]
            most = jnp.where(most < none, most, -1.0)
            for key in keys[1:]:
                most = jnp.maximum(most, jnp.where(key < none, key, -1.0))
            most = jnp.max(most, axis=1, keepdims=True)
            bounds = jnp.where(lane == 2 * j, jnp.floor(least * (1.0 / radial)), bounds)
            bounds = jnp.where(lane == 2 * j + 1, jnp.floor(most * (1.0 / radial)), bounds)
        out_ref[pl.ds(row + slot_rows - 1, 8, stride=slot_rows), :] = bounds
        for i in range(cap_tiles):
            for f in range(fields):
                out_ref[pl.ds(row + base + fields * i + f, 8, stride=slot_rows), :] = tiles[i][f]
        return carry

    lax.fori_loop(0, seg_count // 8, group, 0)


def deposit_kernel(cap_tiles, base, step, got_ref, out_ref, bound_ref, sum_ref, limit_ref, work_ref, sem):
    seg_count, slot_rows, _ = got_ref.shape
    components = out_ref.shape[0]
    azim, radial = out_ref.shape[1:]
    fields = components + 1
    width = step * LANES
    chunk_count = cap_tiles // step
    for s in range(seg_count):
        bound_ref[s : s + 1, :] = got_ref[s, slot_rows - 1 : slot_rows, :].astype(jnp.int32)
    copy = pltpu.make_async_copy(bound_ref, limit_ref, sem)
    copy.start()
    sum_ref[...] = jnp.zeros(sum_ref.shape, jnp.float32)
    cells = lax.broadcasted_iota(jnp.int32, (radial, width), 0).astype(jnp.float32).astype(jnp.bfloat16)
    near = lax.broadcasted_iota(jnp.int32, (WINDOW, width), 0).astype(jnp.float32).astype(jnp.bfloat16)
    copy.wait()

    def listed(s, total):
        for j in range(chunk_count):
            least = limit_ref[s, 2 * j] // 8 * 8
            most = limit_ref[s, 2 * j + 1]

            def add(start, total):
                work_ref[0, total] = s
                work_ref[1, total] = fields * step * j
                work_ref[2, total] = start
                return total + 1

            work_ref[0, total] = s
            work_ref[1, total] = fields * step * j
            work_ref[2, total] = least
            total = jnp.where(most >= 0, total + 1, total)
            total = lax.while_loop(
                lambda c: c[0] <= most,
                lambda c: (c[0] + WINDOW, add(c[0], c[1])),
                (least + WINDOW, total),
            )[1]
        return total

    total = lax.fori_loop(0, seg_count, listed, jnp.int32(0))
    for u in range(UNROLL - 1):
        work_ref[0, total + u] = 0
        work_ref[1, total + u] = 0
        work_ref[2, total + u] = azim

    def product(t):
        s = work_ref[0, t]
        begin = work_ref[1, t]
        start = pl.multiple_of(work_ref[2, t], 8)
        rows = got_ref[s, pl.ds(pl.multiple_of(base + begin, 8 if step % 4 == 0 else 4), fields * step), :]

        def field(k):
            return jnp.concatenate(
                [rows[fields * q + k : fields * q + k + 1] for q in range(step)], axis=1
            )

        ids = field(components)
        a = jnp.floor(ids * (1.0 / radial))
        b = (ids - radial * a).astype(jnp.bfloat16)
        right = jnp.where(cells == b, jnp.bfloat16(1), jnp.bfloat16(0))
        in_a = near == (a - start.astype(jnp.float32)).astype(jnp.bfloat16)
        highs, lows = [], []
        for v in range(components):
            values = field(v)
            high = values.astype(jnp.bfloat16)
            low = (values - high.astype(jnp.float32)).astype(jnp.bfloat16)
            highs.append(jnp.where(in_a, high, jnp.bfloat16(0)))
            lows.append(jnp.where(in_a, low, jnp.bfloat16(0)))
        if WIDE:
            left = jnp.concatenate([jnp.concatenate(highs, axis=0), jnp.concatenate(lows, axis=0)], axis=1)
            part = lax.dot_general(
                left, jnp.concatenate([right, right], axis=1), (((1,), (1,)), ((), ())), preferred_element_type=jnp.float32
            )
        else:
            left = jnp.concatenate(highs + lows, axis=0)
            part = lax.dot_general(
                left, right, (((1,), (1,)), ((), ())), preferred_element_type=jnp.float32
            )
            part = part[: components * WINDOW] + part[components * WINDOW :]
        return start, part

    def several(t, carry):
        done = [product(t * UNROLL + u) for u in range(UNROLL)]
        for start, part in done:
            for v in range(components):
                sum_ref[v, pl.ds(start, WINDOW), :] += part[v * WINDOW : (v + 1) * WINDOW]
        return carry

    lax.fori_loop(0, (total + UNROLL - 1) // UNROLL, several, 0)
    out_ref[...] = sum_ref[:, :azim, :]


def local(state, kappa, drop_src, drop_cell, drop_count, part_map, match_block):
    components, azim_cells, radial_cells = state.shape
    row_count = drop_src.shape[1]
    seg_count = lax.axis_size("segaz")
    capacity = 5 * row_count // (4 * seg_count)
    cap_tiles = capacity // LANES
    step = STEP if cap_tiles % STEP == 0 else 2
    base = 8 * components
    fields = components + 1
    slot_rows = base + 8 + -(-fields * cap_tiles // 8) * 8
    own_index = lax.axis_index("segaz")
    indices = jnp.arange(seg_count, dtype=jnp.int32)
    vmem = pl.BlockSpec(memory_space=pltpu.VMEM)
    smem = pl.BlockSpec(memory_space=pltpu.SMEM)
    sends = pl.pallas_call(
        functools.partial(pack_kernel, cap_tiles, step, base),
        out_shape=jax.ShapeDtypeStruct((seg_count * slot_rows, LANES), jnp.float32),
        in_specs=[smem, vmem, vmem, vmem],
        out_specs=vmem,
        scratch_shapes=[pltpu.VMEM((seg_count // 8, cap_tiles, 64, LANES), jnp.float32)],
        compiler_params=pltpu.CompilerParams(vmem_limit_bytes=48 << 20),
    )(drop_count, drop_src, drop_cell.reshape(-1, LANES), state)
    sends = sends.reshape(seg_count, slot_rows, LANES)
    got = lax.all_to_all(sends, "segaz", split_axis=0, concat_axis=0, tiled=True)
    source = pl.pallas_call(
        functools.partial(deposit_kernel, cap_tiles, base, step),
        out_shape=jax.ShapeDtypeStruct(state.shape, jnp.float32),
        in_specs=[vmem],
        out_specs=vmem,
        scratch_shapes=[
            pltpu.VMEM((seg_count, LANES), jnp.int32),
            pltpu.VMEM((components, azim_cells + WINDOW, radial_cells), jnp.float32),
            pltpu.SMEM((seg_count, LANES), jnp.int32),
            pltpu.SMEM((3, seg_count * (cap_tiles // step) * (azim_cells // WINDOW + 2) + UNROLL), jnp.int32),
            pltpu.SemaphoreType.DMA(()),
        ],
        compiler_params=pltpu.CompilerParams(vmem_limit_bytes=48 << 20),
    )(got)

    padded = extended(state, (("segaz", 1), ("rad", 2)), 1)
    diffusion = kappa[None] * laplace_nine(padded)
    my_block = jnp.sum(jnp.where(indices == own_index, part_map, 0))
    target = jnp.sum(jnp.where(indices == my_block, match_block, 0))
    partner = jnp.sum(jnp.where(part_map == target, indices, 0))
    face_rows = state[:, :JL, :]
    partner_face = lax.dynamic_index_in_dim(got, partner, 0, keepdims=False)[:base]
    partner_face = partner_face.reshape(components, 2, JL, LANES).transpose(0, 2, 1, 3).reshape(face_rows.shape)
    weights = jnp.array(layer_weights, jnp.float32)
    coupling = weights[None, :, None] * (partner_face - face_rows)
    junction = jnp.concatenate(
        [coupling, jnp.zeros((components, azim_cells - JL, radial_cells), jnp.float32)], axis=1
    )
    wide_azim = extended(source, (("segaz", 1),), FW)
    smoothed = smooth_axis(wide_azim, FW, 1, azim_cells)
    wide_radial = extended(smoothed, (("rad", 2),), FW)
    filtered = smooth_axis(wide_radial, FW, 2, radial_cells)
    return state + time_step * (diffusion + junction + filtered)


def solution(mesh):
    return jax.shard_map(
        local,
        mesh=mesh,
        in_specs=(
            P(None, "segaz", "rad"),
            P("segaz", "rad"),
            P(None, ("segaz", "rad")),
            P(("segaz", "rad")),
            P(("segaz", "rad"), None),
            P(),
            P(),
        ),
        out_specs=P(None, "segaz", "rad"),
        check_vma=False,
    )
```

```python
import functools

import jax
import jax.numpy as jnp
import numpy as np
from jax import lax
from jax.experimental import pallas as pl
from jax.experimental.pallas import tpu as pltpu
from jax.sharding import PartitionSpec as P

FW = 4
JL = 4
LANES = 128
WINDOW = 64
ROUNDS = 2
UNROLL = 8
STEP = 4

time_step = 0.25
layer_weights = (1.0, 0.6, 0.35, 0.2)


def filter_weights(half_width):
    offsets = np.arange(-half_width, half_width + 1).astype(np.float32)
    bell_curve = np.exp(-offsets * offsets / np.float32(8.0))
    return bell_curve / np.sum(bell_curve)


def taps(targets, length):
    weights = filter_weights(FW)
    table = np.zeros((len(targets), length), np.float32)
    for i, cell in enumerate(targets):
        if cell is not None:
            for k in range(-FW, FW + 1):
                if 0 <= cell + k < length:
                    table[i, cell + k] = weights[k + FW]
    return table


def edge_targets(length):
    gap = [None] * (8 - FW)
    return list(range(-FW, 0)) + gap + list(range(length, length + FW)) + gap


def extended_targets(length):
    gap = [None] * (LANES - FW)
    return list(range(length)) + gap + list(range(-FW, 0)) + list(range(length, length + FW)) + gap


def pick_columns(radial):
    table = np.zeros((16, 2 * radial), np.float32)
    for k in range(FW):
        table[k, k] = 1.0
        table[8 + k, radial - FW + k] = 1.0
    table[FW, radial] = 1.0
    table[8 + FW, 2 * radial - 1] = 1.0
    return table


def halves(x):
    high = x.astype(jnp.bfloat16)
    return high, (x - high.astype(jnp.float32)).astype(jnp.bfloat16)


def product(x, y, dims):
    xh, xl = halves(x) if not isinstance(x, tuple) else x
    yh, yl = halves(y) if not isinstance(y, tuple) else y

    def dot(p, q):
        return lax.dot_general(p, q, (dims, ((), ())), preferred_element_type=jnp.float32)

    return dot(xh, yh) + (dot(xl, yh) + dot(xh, yl))


PLAIN = ((1,), (0,))
TURNED = ((1,), (1,))


def comparators(count):
    size = 1 << (count - 1).bit_length()
    pairs = []
    p = 1
    while p < size:
        k = p
        while k >= 1:
            for j in range(k % p, size - k, 2 * k):
                for i in range(min(k, size - j - k)):
                    if (i + j) // (2 * p) == (i + j + k) // (2 * p) and i + j + k < count:
                        pairs.append((i + j, i + j + k))
            k //= 2
        p *= 2
    return pairs


def sort_rows(tiles):
    pairs = comparators(len(tiles))
    for low, high in pairs:
        swap = tiles[high][-1] < tiles[low][-1]
        first = [jnp.where(swap, y, x) for x, y in zip(tiles[low], tiles[high])]
        second = [jnp.where(swap, x, y) for x, y in zip(tiles[low], tiles[high])]
        tiles[low], tiles[high] = first, second
    return tiles


def pack_kernel(cap_tiles, step, base, azim, count_ref, src_ref, cell_ref, face_ref, out_ref, held_ref):
    components = src_ref.shape[0]
    fields = components + 1
    tile_count = cell_ref.shape[0]
    radial = face_ref.shape[2]
    slot_rows = base + 8 + -(-fields * cap_tiles // 8) * 8
    seg_count = out_ref.shape[0] // slot_rows
    lane = lax.broadcasted_iota(jnp.int32, (8, LANES), 1)
    sub = lax.broadcasted_iota(jnp.int32, (8, LANES), 0)
    none = float(azim * radial)

    def slot(g, begin):
        count = count_ref[0, g]
        first = begin // LANES
        shift = begin % LANES
        turn = (LANES - shift) % LANES

        def rolled(i):
            t = jnp.minimum(first + i, tile_count - 1)
            src = src_ref[:, pl.ds(pl.multiple_of(t * LANES, LANES), LANES)]
            cell = cell_ref[pl.ds(t, 1), :].astype(jnp.float32)
            both = jnp.concatenate([src, cell, jnp.zeros((8 - fields, LANES), jnp.float32)], axis=0)
            return pltpu.roll(both, turn, 1)

        row = g * slot_rows
        for v in range(components):
            for half in range(2):
                out_ref[pl.ds(row + 8 * v + 4 * half, JL), :] = face_ref[
                    v, 0:JL, half * LANES : (half + 1) * LANES
                ]
        head = rolled(0)
        for i in range(cap_tiles):
            tail = rolled(i + 1)
            rows = jnp.where(lane < LANES - shift, head, tail)
            dead = (sub == components) & (lane >= count - i * LANES)
            rows = jnp.where(dead, none, rows)
            held_ref[g // 8, i, pl.ds(g % 8, 8, stride=8), :] = rows
            head = tail
        return begin + count

    lax.fori_loop(0, seg_count, slot, jnp.int32(0))

    def group(h, carry):
        tiles = [
            [held_ref[h, i, 8 * f : 8 * f + 8, :] for f in range(fields)] for i in range(cap_tiles)
        ]
        tiles = sort_rows(tiles)
        for again in range(ROUNDS - 1):
            tiles = [[pltpu.roll(x, (37 * i) % LANES, 1) for x in tiles[i]] for i in range(cap_tiles)]
            tiles = sort_rows(tiles)
        row = h * 8 * slot_rows
        bounds = jnp.zeros((8, LANES), jnp.float32)
        for j in range(cap_tiles // step):
            keys = [tiles[i][-1] for i in range(step * j, step * j + step)]
            least = jnp.min(keys[0], axis=1, keepdims=True)
            most = keys[0]
            most = jnp.where(most < none, most, -1.0)
            for key in keys[1:]:
                most = jnp.maximum(most, jnp.where(key < none, key, -1.0))
            most = jnp.max(most, axis=1, keepdims=True)
            bounds = jnp.where(lane == 2 * j, jnp.floor(least * (1.0 / radial)), bounds)
            bounds = jnp.where(lane == 2 * j + 1, jnp.floor(most * (1.0 / radial)), bounds)
        out_ref[pl.ds(row + slot_rows - 1, 8, stride=slot_rows), :] = bounds
        for i in range(cap_tiles):
            for f in range(fields):
                out_ref[pl.ds(row + base + fields * i + f, 8, stride=slot_rows), :] = tiles[i][f]
        return carry

    lax.fori_loop(0, seg_count // 8, group, 0)


def base_kernel(state_ref, kappa_ref, out_ref, edge_ref):
    components, azim, radial = state_ref.shape
    lane = lax.broadcasted_iota(jnp.int32, (azim, radial), 1)
    sub = lax.broadcasted_iota(jnp.int32, (8, radial), 0)
    first = lane[:1] == 0
    last = lane[:1] == radial - 1
    pick = lax.broadcasted_iota(jnp.int32, (8, radial), 1)
    pick = ((sub == 2) & (pick == 0)) | ((sub == 3) & (pick == radial - 1))
    pick = jnp.where(pick, 1.0, 0.0).astype(jnp.bfloat16)
    none = jnp.zeros((1, radial), jnp.float32)

    def component(v, carry):
        q = state_ref[v]
        both = jnp.concatenate([q[1:], none], axis=0) + jnp.concatenate([none, q[:-1]], axis=0)
        column = both + 4.0 * q
        side = jnp.where(lane == radial - 1, 0.0, pltpu.roll(column, radial - 1, 1)) + jnp.where(
            lane == 0, 0.0, pltpu.roll(column, 1, 1)
        )
        total = side + (4.0 * both - 20.0 * q)
        out_ref[v] = q + time_step * (kappa_ref[...] * total / 6.0)

        def along(row):
            right = jnp.where(last, 0.0, pltpu.roll(row, radial - 1, 1))
            left = jnp.where(first, 0.0, pltpu.roll(row, 1, 1))
            return 4.0 * row + right + left

        top, bottom = q[:1], q[-1:]
        high, low = halves(column)
        turned = sum(
            lax.dot_general(pick, x, (TURNED, ((), ())), preferred_element_type=jnp.float32) for x in (high, low)
        )
        edge_ref[v] = jnp.where(
            sub == 0,
            along(top),
            jnp.where(sub == 1, along(bottom), jnp.where(sub == 4, top, jnp.where(sub == 5, bottom, turned))),
        )
        return carry

    lax.fori_loop(0, components, component, 0)


def deposit_kernel(
    cap_tiles, base, step,
    map_ref, match_ref, got_ref, face_ref, edge_ref, near_ref, far_ref,
    sum_ref, joint_ref, before_ref, after_ref, side_ref,
    bound_ref, limit_ref, work_ref, sem,
):
    seg_count, slot_rows, _ = got_ref.shape
    components, _, radial = sum_ref.shape
    azim = sum_ref.shape[1] - WINDOW
    fields = components + 1
    width = step * LANES
    chunk_count = cap_tiles // step
    for s in range(seg_count):
        bound_ref[s : s + 1, :] = got_ref[s, slot_rows - 1 : slot_rows, :].astype(jnp.int32)
    copy = pltpu.make_async_copy(bound_ref, limit_ref, sem)
    copy.start()
    sum_ref[...] = jnp.zeros(sum_ref.shape, jnp.float32)
    cells = lax.broadcasted_iota(jnp.int32, (radial, width), 0).astype(jnp.float32).astype(jnp.bfloat16)
    near = lax.broadcasted_iota(jnp.int32, (WINDOW, width), 0).astype(jnp.float32).astype(jnp.bfloat16)
    copy.wait()

    def listed(s, total):
        for j in range(chunk_count):
            least = limit_ref[s, 2 * j] // 8 * 8
            most = limit_ref[s, 2 * j + 1]

            def add(start, total):
                work_ref[0, total] = s
                work_ref[1, total] = fields * step * j
                work_ref[2, total] = start
                return total + 1

            work_ref[0, total] = s
            work_ref[1, total] = fields * step * j
            work_ref[2, total] = least
            total = jnp.where(most >= 0, total + 1, total)
            total = lax.while_loop(
                lambda c: c[0] <= most,
                lambda c: (c[0] + WINDOW, add(c[0], c[1])),
                (least + WINDOW, total),
            )[1]
        return total

    total = lax.fori_loop(0, seg_count, listed, jnp.int32(0))
    for u in range(UNROLL - 1):
        work_ref[0, total + u] = 0
        work_ref[1, total + u] = 0
        work_ref[2, total + u] = azim

    def block(t):
        s = work_ref[0, t]
        begin = work_ref[1, t]
        start = pl.multiple_of(work_ref[2, t], 8)
        rows = got_ref[s, pl.ds(pl.multiple_of(base + begin, 8 if step % 4 == 0 else 4), fields * step), :]

        def field(k):
            return jnp.concatenate(
                [rows[fields * q + k : fields * q + k + 1] for q in range(step)], axis=1
            )

        ids = field(components)
        a = jnp.floor(ids * (1.0 / radial))
        b = (ids - radial * a).astype(jnp.bfloat16)
        right = jnp.where(cells == b, jnp.bfloat16(1), jnp.bfloat16(0))
        in_a = near == (a - start.astype(jnp.float32)).astype(jnp.bfloat16)
        highs, lows = [], []
        for v in range(components):
            values = field(v)
            high = values.astype(jnp.bfloat16)
            low = (values - high.astype(jnp.float32)).astype(jnp.bfloat16)
            highs.append(jnp.where(in_a, high, jnp.bfloat16(0)))
            lows.append(jnp.where(in_a, low, jnp.bfloat16(0)))
        left = jnp.concatenate(highs + lows, axis=0)
        part = lax.dot_general(left, right, (TURNED, ((), ())), preferred_element_type=jnp.float32)
        part = part[: components * WINDOW] + part[components * WINDOW :]
        return start, part

    def several(t, carry):
        done = [block(t * UNROLL + u) for u in range(UNROLL)]
        for start, part in done:
            for v in range(components):
                sum_ref[v, pl.ds(start, WINDOW), :] += part[v * WINDOW : (v + 1) * WINDOW]
        return carry

    lax.fori_loop(0, (total + UNROLL - 1) // UNROLL, several, 0)

    own = lax.axis_index("segaz")
    partner = jnp.int32(0)
    target = match_ref[map_ref[own]]
    for h in range(seg_count):
        partner = jnp.where(map_ref[h] == target, h, partner)
    layer = lax.broadcasted_iota(jnp.int32, (JL, radial), 0)
    strength = jnp.zeros((JL, radial), jnp.float32)
    for l in range(JL):
        strength = jnp.where(layer == l, layer_weights[l], strength)
    for v in range(components):
        tile = got_ref[partner, 8 * v : 8 * v + 8, :]
        face = jnp.concatenate([tile[:JL], tile[JL:]], axis=1)
        joint_ref[v, 0:JL, :] = strength * (face - face_ref[v, 0:JL, :])
        joint_ref[v, JL:8, :] = jnp.zeros((8 - JL, radial), jnp.float32)

    near = halves(near_ref[...])
    far = halves(far_ref[...])
    inner = tuple(x[:, :radial] for x in far)
    rows, columns = [], []
    for v in range(components):
        cells_v = halves(sum_ref[v, 0:azim, :])
        rows.append(product(near, cells_v, PLAIN))
        columns.append(product(near, cells_v, TURNED))
    rows = product(jnp.concatenate(rows, axis=0), inner, PLAIN)
    columns = product(jnp.concatenate(columns, axis=0), far, PLAIN)
    sub = lax.broadcasted_iota(jnp.int32, (8, LANES), 0)
    lane = lax.broadcasted_iota(jnp.int32, (8, LANES), 1)
    half = LANES
    for v in range(components):
        row = rows[16 * v : 16 * v + 16]
        column = columns[16 * v : 16 * v + 16]
        edge = edge_ref[v]
        wide = lax.broadcasted_iota(jnp.int32, (8, radial), 0)
        after_ref[v, :, :radial] = jnp.where(wide == FW, edge[1:2], row[8:16])
        before_ref[v, :, :radial] = jnp.where(
            wide == FW - 1, edge[0:1], jnp.concatenate([row[FW:8], row[0:FW]], axis=0)
        )
        bottom, top = edge[5:6], edge[4:5]
        left_corner = jnp.where(lane[:1] == 0, bottom[:, :half], 0.0)
        right_corner = jnp.where(lane[:1] == 0, pltpu.roll(bottom[:, radial - half :], 1, 1), 0.0)
        after_ref[v, :, radial : radial + half] = jnp.where(
            sub == FW, left_corner, column[0:8, radial + half : radial + 2 * half]
        )
        after_ref[v, :, radial + half : radial + 2 * half] = jnp.where(
            sub == FW, right_corner, column[8:16, radial + half : radial + 2 * half]
        )
        left_corner = jnp.where(lane[:1] == half - 1, pltpu.roll(top[:, :half], half - 1, 1), 0.0)
        right_corner = jnp.where(lane[:1] == half - 1, top[:, radial - half :], 0.0)
        before_ref[v, :, radial : radial + half] = jnp.where(
            sub == FW, left_corner, column[0:8, radial : radial + half]
        )
        before_ref[v, :, radial + half : radial + 2 * half] = jnp.where(
            sub == FW, right_corner, column[8:16, radial : radial + half]
        )
        side_ref[v, 0:8, :] = jnp.where(wide == FW, edge[2:3], column[0:8, :radial])
        side_ref[v, 8:16, :] = jnp.where(wide == FW, edge[3:4], column[8:16, :radial])


def inner_kernel(sum_ref, base_ref, joint_ref, band_ref, out_ref):
    components, azim, radial = base_ref.shape
    band = halves(band_ref[...])

    def component(v, carry):
        across = product(sum_ref[v, 0:azim, :], band, PLAIN)
        both = product(band, across, PLAIN)
        out_ref[v] = base_ref[v] + time_step * both
        out_ref[v, 0:8, :] += time_step * joint_ref[v]
        return carry

    lax.fori_loop(0, components, component, 0)


def corner_kernel(side_ref, prior_ref, next_ref, left_ref, right_ref):
    radial = left_ref.shape[2]
    for out_ref, begin, corner in ((left_ref, 0, radial), (right_ref, 8, radial + LANES)):
        out_ref[:, :, :LANES] = (
            side_ref[:, begin : begin + 8, :LANES] + prior_ref[:, :, corner : corner + LANES]
        )
        out_ref[:, :, LANES:] = (
            side_ref[:, begin : begin + 8, LANES:] + next_ref[:, :, corner : corner + LANES]
        )


def final_kernel(inner_ref, kappa_ref, prior_ref, next_ref, left_ref, right_ref, pick_ref, out_ref):
    components, azim, radial = inner_ref.shape
    pick = pick_ref[...].astype(jnp.bfloat16)
    sub = lax.broadcasted_iota(jnp.int32, (8, radial), 0)

    def component(v, carry):
        parts = halves(jnp.concatenate([left_ref[v], right_ref[v]], axis=0))
        sides = sum(
            lax.dot_general(x, pick, (((0,), (0,)), ((), ())), preferred_element_type=jnp.float32) for x in parts
        )
        kappa = kappa_ref[...]
        out_ref[v] = inner_ref[v] + time_step * (sides[:, :radial] + kappa * sides[:, radial:] / 6.0)
        prior = prior_ref[v, :, :radial]
        add = jnp.where(sub < FW, prior, 0.0) + jnp.where(
            sub == 0, kappa[0:8] * prior[FW : FW + 1] / 6.0, 0.0
        )
        out_ref[v, 0:8, :] += time_step * add
        nxt = next_ref[v, :, :radial]
        add = jnp.where(sub >= 8 - FW, nxt, 0.0) + jnp.where(
            sub == 7, kappa[azim - 8 : azim] * nxt[FW - 1 : FW] / 6.0, 0.0
        )
        out_ref[v, azim - 8 : azim, :] += time_step * add
        return carry

    lax.fori_loop(0, components, component, 0)


def call(kernel, outs, ins, scratch=(), cost=None):
    def spec(where):
        if where == "smem":
            return pl.BlockSpec(memory_space=pltpu.SMEM)
        if where == "vmem":
            return pl.BlockSpec(memory_space=pltpu.VMEM)
        return pl.BlockSpec(where, lambda i: (0,) * len(where))

    return pl.pallas_call(
        kernel,
        grid=(1,),
        out_shape=[jax.ShapeDtypeStruct(shape, jnp.float32) for shape in outs],
        in_specs=[spec(where) for where in ins],
        out_specs=[pl.BlockSpec(memory_space=pltpu.VMEM)] * len(outs),
        scratch_shapes=list(scratch),
        cost_estimate=None
        if cost is None
        else pl.CostEstimate(flops=cost, bytes_accessed=cost // 1000, transcendentals=0),
        compiler_params=pltpu.CompilerParams(vmem_limit_bytes=48 << 20),
    )


def shifted(strip, axis, way):
    count = lax.axis_size(axis)
    pairs = [(i, i + 1) if way > 0 else (i + 1, i) for i in range(count - 1)]
    return lax.ppermute(strip, axis, pairs)


def local(state, kappa, drop_src, drop_cell, drop_count, part_map, match_block):
    components, azim, radial = state.shape
    row_count = drop_src.shape[1]
    seg_count = lax.axis_size("segaz")
    capacity = 5 * row_count // (4 * seg_count)
    cap_tiles = capacity // LANES
    step = STEP if cap_tiles % STEP == 0 else 2
    base = 8 * components
    fields = components + 1
    slot_rows = base + 8 + -(-fields * cap_tiles // 8) * 8
    items = seg_count * (cap_tiles // step) * (azim // WINDOW + 2) + UNROLL
    face = (components, 8, radial)
    whole = state.shape
    strip = (components, 8, 2 * radial)
    sides = (components, 8, radial)
    (sends,) = call(
        functools.partial(pack_kernel, cap_tiles, step, base, azim),
        [(seg_count * slot_rows, LANES)],
        ["smem", "vmem", "vmem", face],
        [pltpu.VMEM((seg_count // 8, cap_tiles, 64, LANES), jnp.float32)],
    )(drop_count, drop_src, drop_cell.reshape(-1, LANES), state)
    got = lax.all_to_all(
        sends.reshape(seg_count, slot_rows, LANES), "segaz", split_axis=0, concat_axis=0, tiled=True
    )
    still, edge = call(base_kernel, [whole, face], ["vmem", "vmem"], cost=1 << 22)(state, kappa)
    near = jnp.asarray(taps(edge_targets(azim), azim))
    far = jnp.asarray(taps(extended_targets(azim), azim).T)
    band = jnp.asarray(taps(list(range(azim)), azim))
    source, joint, before, after, side = call(
        functools.partial(deposit_kernel, cap_tiles, base, step),
        [(components, azim + WINDOW, radial), face, strip, strip, (components, 16, radial)],
        ["smem", "smem", "vmem", face, "vmem", "vmem", "vmem"],
        [
            pltpu.VMEM((seg_count, LANES), jnp.int32),
            pltpu.SMEM((seg_count, LANES), jnp.int32),
            pltpu.SMEM((3, items), jnp.int32),
            pltpu.SemaphoreType.DMA(()),
        ],
    )(part_map, match_block, got, state, edge, near, far)
    prior = shifted(after, "segaz", 1)
    nxt = shifted(before, "segaz", -1)
    (inner,) = call(inner_kernel, [whole], ["vmem"] * 4, cost=1 << 22)(source, still, joint, band)
    to_left, to_right = call(corner_kernel, [sides, sides], ["vmem"] * 3)(side, prior, nxt)
    left = shifted(to_right, "rad", 1)
    right = shifted(to_left, "rad", -1)
    pick = jnp.asarray(pick_columns(radial))
    (result,) = call(final_kernel, [whole], ["vmem"] * 7)(inner, kappa, prior, nxt, left, right, pick)
    return result


def solution(mesh):
    return jax.shard_map(
        local,
        mesh=mesh,
        in_specs=(
            P(None, "segaz", "rad"),
            P("segaz", "rad"),
            P(None, ("segaz", "rad")),
            P(("segaz", "rad")),
            P(("segaz", "rad"), None),
            P(),
            P(),
        ),
        out_specs=P(None, "segaz", "rad"),
        check_vma=False,
    )
```

```python
import functools

import jax
import jax.numpy as jnp
import numpy as np
from jax import lax
from jax.experimental import pallas as pl
from jax.experimental.pallas import tpu as pltpu
from jax.sharding import PartitionSpec as P

FW = 4
JL = 4
LANES = 128
WINDOW = 64
ROUNDS = 2
UNROLL = 8
STEP = 4
PIECES = 4

time_step = 0.25
layer_weights = (1.0, 0.6, 0.35, 0.2)


def filter_weights(half_width):
    offsets = np.arange(-half_width, half_width + 1).astype(np.float32)
    bell_curve = np.exp(-offsets * offsets / np.float32(8.0))
    return bell_curve / np.sum(bell_curve)


def taps(targets, length):
    weights = filter_weights(FW)
    table = np.zeros((len(targets), length), np.float32)
    for i, cell in enumerate(targets):
        if cell is not None:
            for k in range(-FW, FW + 1):
                if 0 <= cell + k < length:
                    table[i, cell + k] = weights[k + FW]
    return table


def edge_targets(length):
    gap = [None] * (8 - FW)
    return list(range(-FW, 0)) + gap + list(range(length, length + FW)) + gap


def extended_targets(length):
    gap = [None] * (LANES - FW)
    return list(range(length)) + gap + list(range(-FW, 0)) + list(range(length, length + FW)) + gap


def pick_columns(radial):
    table = np.zeros((16, 2 * radial), np.float32)
    for k in range(FW):
        table[k, k] = 1.0
        table[8 + k, radial - FW + k] = 1.0
    table[FW, radial] = 1.0
    table[8 + FW, 2 * radial - 1] = 1.0
    return table


def halves(x):
    high = x.astype(jnp.bfloat16)
    return high, (x - high.astype(jnp.float32)).astype(jnp.bfloat16)


def product(x, y, dims):
    xh, xl = halves(x) if not isinstance(x, tuple) else x
    yh, yl = halves(y) if not isinstance(y, tuple) else y

    def dot(p, q):
        return lax.dot_general(p, q, (dims, ((), ())), preferred_element_type=jnp.float32)

    return dot(xh, yh) + (dot(xl, yh) + dot(xh, yl))


PLAIN = ((1,), (0,))
TURNED = ((1,), (1,))


def comparators(count):
    size = 1 << (count - 1).bit_length()
    pairs = []
    p = 1
    while p < size:
        k = p
        while k >= 1:
            for j in range(k % p, size - k, 2 * k):
                for i in range(min(k, size - j - k)):
                    if (i + j) // (2 * p) == (i + j + k) // (2 * p) and i + j + k < count:
                        pairs.append((i + j, i + j + k))
            k //= 2
        p *= 2
    return pairs


def sort_rows(tiles):
    pairs = comparators(len(tiles))
    for low, high in pairs:
        swap = tiles[high][-1] < tiles[low][-1]
        first = [jnp.where(swap, y, x) for x, y in zip(tiles[low], tiles[high])]
        second = [jnp.where(swap, x, y) for x, y in zip(tiles[low], tiles[high])]
        tiles[low], tiles[high] = first, second
    return tiles


def pack_kernel(
    cap_tiles, step, base, azim,
    count_hbm, src_hbm, cell_hbm, state_hbm, sends_hbm,
    count_ref, src_ref, cell_ref, face_ref, out_ref, held_ref, in_sems, out_sems,
):
    components, row_count = src_ref.shape
    fields = components + 1
    tile_count = cell_ref.shape[0]
    radial = face_ref.shape[2]
    seg_count, slot_rows, _ = sends_hbm.shape
    piece = row_count // PIECES
    loads = [
        pltpu.make_async_copy(count_hbm, count_ref, in_sems.at[0]),
        pltpu.make_async_copy(state_hbm.at[:, 0:8, :], face_ref, in_sems.at[1]),
        pltpu.make_async_copy(cell_hbm, cell_ref, in_sems.at[2]),
    ] + [
        pltpu.make_async_copy(
            src_hbm.at[:, k * piece : (k + 1) * piece], src_ref.at[:, k * piece : (k + 1) * piece], in_sems.at[3 + k]
        )
        for k in range(PIECES)
    ]
    for load in loads:
        load.start()
    for load in loads:
        load.wait()
    lane = lax.broadcasted_iota(jnp.int32, (8, LANES), 1)
    sub = lax.broadcasted_iota(jnp.int32, (8, LANES), 0)
    none = float(azim * radial)

    def slot(g, begin):
        count = count_ref[0, g]
        first = begin // LANES
        shift = begin % LANES
        turn = (LANES - shift) % LANES

        def rolled(i):
            t = jnp.minimum(first + i, tile_count - 1)
            src = src_ref[:, pl.ds(pl.multiple_of(t * LANES, LANES), LANES)]
            cell = cell_ref[pl.ds(t, 1), :].astype(jnp.float32)
            both = jnp.concatenate([src, cell, jnp.zeros((8 - fields, LANES), jnp.float32)], axis=0)
            return pltpu.roll(both, turn, 1)

        row = g * slot_rows
        for v in range(components):
            for half in range(2):
                out_ref[pl.ds(row + 8 * v + 4 * half, JL), :] = face_ref[
                    v, 0:JL, half * LANES : (half + 1) * LANES
                ]
        head = rolled(0)
        for i in range(cap_tiles):
            tail = rolled(i + 1)
            rows = jnp.where(lane < LANES - shift, head, tail)
            dead = (sub == components) & (lane >= count - i * LANES)
            rows = jnp.where(dead, none, rows)
            held_ref[g // 8, i, pl.ds(g % 8, 8, stride=8), :] = rows
            head = tail
        return begin + count

    lax.fori_loop(0, seg_count, slot, jnp.int32(0))

    def group(h):
        tiles = [
            [held_ref[h, i, 8 * f : 8 * f + 8, :] for f in range(fields)] for i in range(cap_tiles)
        ]
        tiles = sort_rows(tiles)
        for again in range(ROUNDS - 1):
            tiles = [[pltpu.roll(x, (37 * i) % LANES, 1) for x in tiles[i]] for i in range(cap_tiles)]
            tiles = sort_rows(tiles)
        row = h * 8 * slot_rows
        bounds = jnp.zeros((8, LANES), jnp.float32)
        for j in range(cap_tiles // step):
            keys = [tiles[i][-1] for i in range(step * j, step * j + step)]
            least = jnp.min(keys[0], axis=1, keepdims=True)
            most = keys[0]
            most = jnp.where(most < none, most, -1.0)
            for key in keys[1:]:
                most = jnp.maximum(most, jnp.where(key < none, key, -1.0))
            most = jnp.max(most, axis=1, keepdims=True)
            bounds = jnp.where(lane == 2 * j, jnp.floor(least * (1.0 / radial)), bounds)
            bounds = jnp.where(lane == 2 * j + 1, jnp.floor(most * (1.0 / radial)), bounds)
        out_ref[pl.ds(row + slot_rows - 1, 8, stride=slot_rows), :] = bounds
        for i in range(cap_tiles):
            for f in range(fields):
                out_ref[pl.ds(row + base + fields * i + f, 8, stride=slot_rows), :] = tiles[i][f]

    stores = []
    for h in range(seg_count // 8):
        group(h)
        for g in range(8 * h, 8 * h + 8):
            store = pltpu.make_async_copy(
                out_ref.at[g * slot_rows : (g + 1) * slot_rows, :], sends_hbm.at[g], out_sems.at[g]
            )
            store.start()
            stores.append(store)
    for store in stores:
        store.wait()


def base_kernel(state_ref, kappa_ref, out_ref, edge_ref):
    components, azim, radial = state_ref.shape
    lane = lax.broadcasted_iota(jnp.int32, (azim, radial), 1)
    sub = lax.broadcasted_iota(jnp.int32, (8, radial), 0)
    first = lane[:1] == 0
    last = lane[:1] == radial - 1
    pick = lax.broadcasted_iota(jnp.int32, (8, radial), 1)
    pick = ((sub == 2) & (pick == 0)) | ((sub == 3) & (pick == radial - 1))
    pick = jnp.where(pick, 1.0, 0.0).astype(jnp.bfloat16)
    none = jnp.zeros((1, radial), jnp.float32)

    def component(v, carry):
        q = state_ref[v]
        both = jnp.concatenate([q[1:], none], axis=0) + jnp.concatenate([none, q[:-1]], axis=0)
        column = both + 4.0 * q
        side = jnp.where(lane == radial - 1, 0.0, pltpu.roll(column, radial - 1, 1)) + jnp.where(
            lane == 0, 0.0, pltpu.roll(column, 1, 1)
        )
        total = side + (4.0 * both - 20.0 * q)
        out_ref[v] = q + time_step * (kappa_ref[...] * total / 6.0)

        def along(row):
            right = jnp.where(last, 0.0, pltpu.roll(row, radial - 1, 1))
            left = jnp.where(first, 0.0, pltpu.roll(row, 1, 1))
            return 4.0 * row + right + left

        top, bottom = q[:1], q[-1:]
        high, low = halves(column)
        turned = sum(
            lax.dot_general(pick, x, (TURNED, ((), ())), preferred_element_type=jnp.float32) for x in (high, low)
        )
        edge_ref[v] = jnp.where(
            sub == 0,
            along(top),
            jnp.where(sub == 1, along(bottom), jnp.where(sub == 4, top, jnp.where(sub == 5, bottom, turned))),
        )
        return carry

    lax.fori_loop(0, components, component, 0)


def deposit_kernel(
    cap_tiles, base, step,
    map_ref, match_ref, got_ref, face_ref, edge_ref, near_ref, far_ref,
    sum_ref, joint_ref, before_ref, after_ref, side_ref,
    bound_ref, limit_ref, work_ref, sem,
):
    seg_count, slot_rows, _ = got_ref.shape
    components, _, radial = sum_ref.shape
    azim = sum_ref.shape[1] - WINDOW
    fields = components + 1
    width = step * LANES
    chunk_count = cap_tiles // step
    for s in range(seg_count):
        bound_ref[s : s + 1, :] = got_ref[s, slot_rows - 1 : slot_rows, :].astype(jnp.int32)
    copy = pltpu.make_async_copy(bound_ref, limit_ref, sem)
    copy.start()
    sum_ref[...] = jnp.zeros(sum_ref.shape, jnp.float32)
    cells = lax.broadcasted_iota(jnp.int32, (radial, width), 0).astype(jnp.float32).astype(jnp.bfloat16)
    near = lax.broadcasted_iota(jnp.int32, (WINDOW, width), 0).astype(jnp.float32).astype(jnp.bfloat16)
    copy.wait()

    def listed(s, total):
        for j in range(chunk_count):
            least = limit_ref[s, 2 * j] // 8 * 8
            most = limit_ref[s, 2 * j + 1]

            def add(start, total):
                work_ref[0, total] = s
                work_ref[1, total] = fields * step * j
                work_ref[2, total] = start
                return total + 1

            work_ref[0, total] = s
            work_ref[1, total] = fields * step * j
            work_ref[2, total] = least
            total = jnp.where(most >= 0, total + 1, total)
            total = lax.while_loop(
                lambda c: c[0] <= most,
                lambda c: (c[0] + WINDOW, add(c[0], c[1])),
                (least + WINDOW, total),
            )[1]
        return total

    total = lax.fori_loop(0, seg_count, listed, jnp.int32(0))
    for u in range(UNROLL - 1):
        work_ref[0, total + u] = 0
        work_ref[1, total + u] = 0
        work_ref[2, total + u] = azim

    def block(t):
        s = work_ref[0, t]
        begin = work_ref[1, t]
        start = pl.multiple_of(work_ref[2, t], 8)
        rows = got_ref[s, pl.ds(pl.multiple_of(base + begin, 8 if step % 4 == 0 else 4), fields * step), :]

        def field(k):
            return jnp.concatenate(
                [rows[fields * q + k : fields * q + k + 1] for q in range(step)], axis=1
            )

        ids = field(components)
        a = jnp.floor(ids * (1.0 / radial))
        b = (ids - radial * a).astype(jnp.bfloat16)
        right = jnp.where(cells == b, jnp.bfloat16(1), jnp.bfloat16(0))
        in_a = near == (a - start.astype(jnp.float32)).astype(jnp.bfloat16)
        highs, lows = [], []
        for v in range(components):
            values = field(v)
            high = values.astype(jnp.bfloat16)
            low = (values - high.astype(jnp.float32)).astype(jnp.bfloat16)
            highs.append(jnp.where(in_a, high, jnp.bfloat16(0)))
            lows.append(jnp.where(in_a, low, jnp.bfloat16(0)))
        left = jnp.concatenate(highs + lows, axis=0)
        part = lax.dot_general(left, right, (TURNED, ((), ())), preferred_element_type=jnp.float32)
        part = part[: components * WINDOW] + part[components * WINDOW :]
        return start, part

    def several(t, carry):
        done = [block(t * UNROLL + u) for u in range(UNROLL)]
        for start, part in done:
            for v in range(components):
                sum_ref[v, pl.ds(start, WINDOW), :] += part[v * WINDOW : (v + 1) * WINDOW]
        return carry

    lax.fori_loop(0, (total + UNROLL - 1) // UNROLL, several, 0)

    own = lax.axis_index("segaz")
    partner = jnp.int32(0)
    target = match_ref[map_ref[own]]
    for h in range(seg_count):
        partner = jnp.where(map_ref[h] == target, h, partner)
    layer = lax.broadcasted_iota(jnp.int32, (JL, radial), 0)
    strength = jnp.zeros((JL, radial), jnp.float32)
    for l in range(JL):
        strength = jnp.where(layer == l, layer_weights[l], strength)
    for v in range(components):
        tile = got_ref[partner, 8 * v : 8 * v + 8, :]
        face = jnp.concatenate([tile[:JL], tile[JL:]], axis=1)
        joint_ref[v, 0:JL, :] = strength * (face - face_ref[v, 0:JL, :])
        joint_ref[v, JL:8, :] = jnp.zeros((8 - JL, radial), jnp.float32)

    near = halves(near_ref[...])
    far = halves(far_ref[...])
    inner = tuple(x[:, :radial] for x in far)
    rows, columns = [], []
    for v in range(components):
        cells_v = halves(sum_ref[v, 0:azim, :])
        rows.append(product(near, cells_v, PLAIN))
        columns.append(product(near, cells_v, TURNED))
    rows = product(jnp.concatenate(rows, axis=0), inner, PLAIN)
    columns = product(jnp.concatenate(columns, axis=0), far, PLAIN)
    sub = lax.broadcasted_iota(jnp.int32, (8, LANES), 0)
    lane = lax.broadcasted_iota(jnp.int32, (8, LANES), 1)
    half = LANES
    for v in range(components):
        row = rows[16 * v : 16 * v + 16]
        column = columns[16 * v : 16 * v + 16]
        edge = edge_ref[v]
        wide = lax.broadcasted_iota(jnp.int32, (8, radial), 0)
        after_ref[v, :, :radial] = jnp.where(wide == FW, edge[1:2], row[8:16])
        before_ref[v, :, :radial] = jnp.where(
            wide == FW - 1, edge[0:1], jnp.concatenate([row[FW:8], row[0:FW]], axis=0)
        )
        bottom, top = edge[5:6], edge[4:5]
        left_corner = jnp.where(lane[:1] == 0, bottom[:, :half], 0.0)
        right_corner = jnp.where(lane[:1] == 0, pltpu.roll(bottom[:, radial - half :], 1, 1), 0.0)
        after_ref[v, :, radial : radial + half] = jnp.where(
            sub == FW, left_corner, column[0:8, radial + half : radial + 2 * half]
        )
        after_ref[v, :, radial + half : radial + 2 * half] = jnp.where(
            sub == FW, right_corner, column[8:16, radial + half : radial + 2 * half]
        )
        left_corner = jnp.where(lane[:1] == half - 1, pltpu.roll(top[:, :half], half - 1, 1), 0.0)
        right_corner = jnp.where(lane[:1] == half - 1, top[:, radial - half :], 0.0)
        before_ref[v, :, radial : radial + half] = jnp.where(
            sub == FW, left_corner, column[0:8, radial : radial + half]
        )
        before_ref[v, :, radial + half : radial + 2 * half] = jnp.where(
            sub == FW, right_corner, column[8:16, radial : radial + half]
        )
        side_ref[v, 0:8, :] = jnp.where(wide == FW, edge[2:3], column[0:8, :radial])
        side_ref[v, 8:16, :] = jnp.where(wide == FW, edge[3:4], column[8:16, :radial])


def inner_kernel(sum_ref, base_ref, joint_ref, band_ref, out_ref):
    components, azim, radial = base_ref.shape
    band = halves(band_ref[...])

    def component(v, carry):
        across = product(sum_ref[v, 0:azim, :], band, PLAIN)
        both = product(band, across, PLAIN)
        out_ref[v] = base_ref[v] + time_step * both
        out_ref[v, 0:8, :] += time_step * joint_ref[v]
        return carry

    lax.fori_loop(0, components, component, 0)


def corner_kernel(inner_ref, side_ref, prior_ref, next_ref, left_ref, right_ref):
    radial = left_ref.shape[2]
    for out_ref, begin, corner in ((left_ref, 0, radial), (right_ref, 8, radial + LANES)):
        out_ref[:, :, :LANES] = (
            side_ref[:, begin : begin + 8, :LANES] + prior_ref[:, :, corner : corner + LANES]
        )
        out_ref[:, :, LANES:] = (
            side_ref[:, begin : begin + 8, LANES:] + next_ref[:, :, corner : corner + LANES]
        )


def final_kernel(inner_ref, kappa_ref, prior_ref, next_ref, left_ref, right_ref, pick_ref, out_ref):
    v = pl.program_id(0)
    azim, radial = kappa_ref.shape
    pick = pick_ref[...].astype(jnp.bfloat16)
    sub = lax.broadcasted_iota(jnp.int32, (8, radial), 0)
    parts = halves(jnp.concatenate([left_ref[v], right_ref[v]], axis=0))
    sides = sum(
        lax.dot_general(x, pick, (((0,), (0,)), ((), ())), preferred_element_type=jnp.float32) for x in parts
    )
    kappa = kappa_ref[...]
    out_ref[0] = inner_ref[v] + time_step * (sides[:, :radial] + kappa * sides[:, radial:] / 6.0)
    prior = prior_ref[v, :, :radial]
    add = jnp.where(sub < FW, prior, 0.0) + jnp.where(sub == 0, kappa[0:8] * prior[FW : FW + 1] / 6.0, 0.0)
    out_ref[0, 0:8, :] += time_step * add
    nxt = next_ref[v, :, :radial]
    add = jnp.where(sub >= 8 - FW, nxt, 0.0) + jnp.where(
        sub == 7, kappa[azim - 8 : azim] * nxt[FW - 1 : FW] / 6.0, 0.0
    )
    out_ref[0, azim - 8 : azim, :] += time_step * add


def call(kernel, outs, ins, scratch=(), cost=None, to="vmem", room=48):
    spaces = {"smem": pltpu.SMEM, "vmem": pltpu.VMEM, "hbm": pltpu.HBM, "any": pl.ANY}

    def spec(where):
        if isinstance(where, str):
            return pl.BlockSpec(memory_space=spaces[where])
        return pl.BlockSpec(where, lambda i: (0,) * len(where))

    return pl.pallas_call(
        kernel,
        grid=(1,),
        out_shape=[jax.ShapeDtypeStruct(shape, jnp.float32) for shape in outs],
        in_specs=[spec(where) for where in ins],
        out_specs=[spec(to)] * len(outs),
        scratch_shapes=list(scratch),
        cost_estimate=None
        if cost is None
        else pl.CostEstimate(flops=cost, bytes_accessed=cost // 1000, transcendentals=0),
        compiler_params=pltpu.CompilerParams(vmem_limit_bytes=room << 20),
    )


def shifted(strip, axis, way):
    count = lax.axis_size(axis)
    pairs = [(i, i + 1) if way > 0 else (i + 1, i) for i in range(count - 1)]
    return lax.ppermute(strip, axis, pairs)


def local(state, kappa, drop_src, drop_cell, drop_count, part_map, match_block):
    components, azim, radial = state.shape
    row_count = drop_src.shape[1]
    seg_count = lax.axis_size("segaz")
    capacity = 5 * row_count // (4 * seg_count)
    cap_tiles = capacity // LANES
    step = STEP if cap_tiles % STEP == 0 else 2
    base = 8 * components
    fields = components + 1
    slot_rows = base + 8 + -(-fields * cap_tiles // 8) * 8
    items = seg_count * (cap_tiles // step) * (azim // WINDOW + 2) + UNROLL
    face = (components, 8, radial)
    whole = state.shape
    strip = (components, 8, 2 * radial)
    sides = (components, 8, radial)
    (sends,) = call(
        functools.partial(pack_kernel, cap_tiles, step, base, azim),
        [(seg_count, slot_rows, LANES)],
        ["hbm"] * 4,
        [
            pltpu.SMEM(drop_count.shape[:1] + (seg_count,), jnp.int32),
            pltpu.VMEM(drop_src.shape, jnp.float32),
            pltpu.VMEM((row_count // LANES, LANES), jnp.int32),
            pltpu.VMEM(face, jnp.float32),
            pltpu.VMEM((seg_count * slot_rows, LANES), jnp.float32),
            pltpu.VMEM((seg_count // 8, cap_tiles, 64, LANES), jnp.float32),
            pltpu.SemaphoreType.DMA((3 + PIECES,)),
            pltpu.SemaphoreType.DMA((seg_count,)),
        ],
        to="hbm",
        room=62,
    )(drop_count, drop_src, drop_cell.reshape(-1, LANES), state)
    got = lax.all_to_all(sends, "segaz", split_axis=0, concat_axis=0, tiled=True)
    still, edge = call(base_kernel, [whole, face], ["vmem", "vmem"], cost=1 << 22)(state, kappa)
    near = jnp.asarray(taps(edge_targets(azim), azim))
    far = jnp.asarray(taps(extended_targets(azim), azim).T)
    band = jnp.asarray(taps(list(range(azim)), azim))
    source, joint, before, after, side = call(
        functools.partial(deposit_kernel, cap_tiles, base, step),
        [(components, azim + WINDOW, radial), face, strip, strip, (components, 16, radial)],
        ["smem", "smem", "vmem", face, "vmem", "vmem", "vmem"],
        [
            pltpu.VMEM((seg_count, LANES), jnp.int32),
            pltpu.SMEM((seg_count, LANES), jnp.int32),
            pltpu.SMEM((3, items), jnp.int32),
            pltpu.SemaphoreType.DMA(()),
        ],
    )(part_map, match_block, got, state, edge, near, far)
    prior = shifted(after, "segaz", 1)
    nxt = shifted(before, "segaz", -1)
    (inner,) = call(inner_kernel, [whole], ["vmem"] * 4, cost=1 << 22)(source, still, joint, band)
    to_left, to_right = call(corner_kernel, [sides, sides], ["any"] + ["vmem"] * 3)(inner, side, prior, nxt)
    left = shifted(to_right, "rad", 1)
    right = shifted(to_left, "rad", -1)
    pick = jnp.asarray(pick_columns(radial))
    return pl.pallas_call(
        final_kernel,
        grid=(components,),
        out_shape=jax.ShapeDtypeStruct(whole, jnp.float32),
        in_specs=[pl.BlockSpec(memory_space=pltpu.VMEM)] * 7,
        out_specs=pl.BlockSpec((1, azim, radial), lambda v: (v, 0, 0)),
        compiler_params=pltpu.CompilerParams(vmem_limit_bytes=48 << 20),
    )(inner, kappa, prior, nxt, left, right, pick)


def solution(mesh):
    return jax.shard_map(
        local,
        mesh=mesh,
        in_specs=(
            P(None, "segaz", "rad"),
            P("segaz", "rad"),
            P(None, ("segaz", "rad")),
            P(("segaz", "rad")),
            P(("segaz", "rad"), None),
            P(),
            P(),
        ),
        out_specs=P(None, "segaz", "rad"),
        check_vma=False,
    )
```

```python
import functools

import jax
import jax.numpy as jnp
import numpy as np
from jax import lax
from jax.experimental import pallas as pl
from jax.experimental.pallas import tpu as pltpu
from jax.sharding import PartitionSpec as P

FW = 4
JL = 4
LANES = 128
WINDOW = 32
ROUNDS = 3
UNROLL = 16
OWN_UNROLL = 5
STEP = 4
PIECES = 4
HALF = 64

time_step = 0.25
layer_weights = (1.0, 0.6, 0.35, 0.2)


def filter_weights(half_width):
    offsets = np.arange(-half_width, half_width + 1).astype(np.float32)
    bell_curve = np.exp(-offsets * offsets / np.float32(8.0))
    return bell_curve / np.sum(bell_curve)


def taps(targets, length):
    weights = filter_weights(FW)
    table = np.zeros((len(targets), length), np.float32)
    for i, cell in enumerate(targets):
        if cell is not None:
            for k in range(-FW, FW + 1):
                if 0 <= cell + k < length:
                    table[i, cell + k] = weights[k + FW]
    return table


def edge_targets(length):
    gap = [None] * (8 - FW)
    return list(range(-FW, 0)) + gap + list(range(length, length + FW)) + gap


def extended_targets(length):
    gap = [None] * (LANES - FW)
    return list(range(length)) + gap + list(range(-FW, 0)) + list(range(length, length + FW)) + gap


def pick_columns(radial):
    table = np.zeros((16, 2 * radial), np.float32)
    for k in range(FW):
        table[k, k] = 1.0
        table[8 + k, radial - FW + k] = 1.0
    table[FW, radial] = 1.0
    table[8 + FW, 2 * radial - 1] = 1.0
    return table


def halves(x):
    high = x.astype(jnp.bfloat16)
    return high, (x - high.astype(jnp.float32)).astype(jnp.bfloat16)


def product(x, y, dims):
    xh, xl = halves(x) if not isinstance(x, tuple) else x
    yh, yl = halves(y) if not isinstance(y, tuple) else y

    def dot(p, q):
        return lax.dot_general(p, q, (dims, ((), ())), preferred_element_type=jnp.float32)

    both = dot(jnp.concatenate([xh, xl], axis=0), yh)
    count = xh.shape[0]
    return both[:count] + (both[count:] + dot(xh, yl))


PLAIN = ((1,), (0,))
TURNED = ((1,), (1,))


def comparators(count):
    size = 1 << (count - 1).bit_length()
    pairs = []
    p = 1
    while p < size:
        k = p
        while k >= 1:
            for j in range(k % p, size - k, 2 * k):
                for i in range(min(k, size - j - k)):
                    if (i + j) // (2 * p) == (i + j + k) // (2 * p) and i + j + k < count:
                        pairs.append((i + j, i + j + k))
            k //= 2
        p *= 2
    return pairs


def sort_rows(tiles):
    pairs = comparators(len(tiles))
    for low, high in pairs:
        swap = tiles[high][-1] < tiles[low][-1]
        first = [jnp.where(swap, y, x) for x, y in zip(tiles[low], tiles[high])]
        second = [jnp.where(swap, x, y) for x, y in zip(tiles[low], tiles[high])]
        tiles[low], tiles[high] = first, second
    return tiles


class Slots:
    def __init__(self, components, cap_tiles, step):
        self.fields = components + 1
        self.cap_tiles, self.step = cap_tiles, step
        self.chunks = cap_tiles // step
        self.chunk_rows = self.fields * step
        self.face = -(-(8 + self.chunks * self.chunk_rows) // 8) * 8
        self.rows = self.face + 8 * components

    def place(self, j):
        return 8 + j * self.chunk_rows


def pack_kernel(
    slots, azim,
    count_hbm, src_hbm, cell_hbm, state_hbm, *refs,
):
    sends_hbm, count_ref, src_ref, cell_ref, face_ref, out_ref, held_ref, in_sems, out_sems = refs
    cap_tiles, step = slots.cap_tiles, slots.step
    components, row_count = src_ref.shape
    fields = components + 1
    tile_count = cell_ref.shape[0]
    radial = face_ref.shape[2]
    seg_count = sends_hbm.shape[0]
    piece = row_count // PIECES
    loads = [
        pltpu.make_async_copy(count_hbm, count_ref, in_sems.at[0]),
        pltpu.make_async_copy(state_hbm.at[:, 0:8, :], face_ref, in_sems.at[1]),
        pltpu.make_async_copy(cell_hbm, cell_ref, in_sems.at[2]),
    ] + [
        pltpu.make_async_copy(
            src_hbm.at[:, k * piece : (k + 1) * piece], src_ref.at[:, k * piece : (k + 1) * piece], in_sems.at[3 + k]
        )
        for k in range(PIECES)
    ]
    for load in loads:
        load.start()
    for load in loads:
        load.wait()
    lane = lax.broadcasted_iota(jnp.int32, (8, LANES), 1)
    sub = lax.broadcasted_iota(jnp.int32, (8, LANES), 0)
    none = float(azim * radial)

    def slot(g, begin):
        count = count_ref[0, g]
        first = begin // LANES
        shift = begin % LANES
        turn = (LANES - shift) % LANES

        def rolled(i):
            t = jnp.minimum(first + i, tile_count - 1)
            src = src_ref[:, pl.ds(pl.multiple_of(t * LANES, LANES), LANES)]
            cell = cell_ref[pl.ds(t, 1), :].astype(jnp.float32)
            both = jnp.concatenate([src, cell, jnp.zeros((8 - fields, LANES), jnp.float32)], axis=0)
            return pltpu.roll(both, turn, 1)

        row = g * slots.rows + slots.face
        for v in range(components):
            for half in range(2):
                out_ref[pl.ds(row + 8 * v + 4 * half, JL), :] = face_ref[
                    v, 0:JL, half * LANES : (half + 1) * LANES
                ]
        head = rolled(0)
        for i in range(cap_tiles):
            tail = rolled(i + 1)
            rows = jnp.where(lane < LANES - shift, head, tail)
            dead = (sub == components) & (lane >= count - i * LANES)
            rows = jnp.where(dead, none, rows)
            held_ref[g // 8, i, pl.ds(g % 8, 8, stride=8), :] = rows
            head = tail
        return begin + count

    lax.fori_loop(0, seg_count, slot, jnp.int32(0))

    def group(h):
        tiles = [
            [held_ref[h, i, 8 * f : 8 * f + 8, :] for f in range(fields)] for i in range(cap_tiles)
        ]
        tiles = sort_rows(tiles)
        for again in range(ROUNDS - 1):
            tiles = [[pltpu.roll(x, (37 * i) % LANES, 1) for x in tiles[i]] for i in range(cap_tiles)]
            tiles = sort_rows(tiles)
        bounds = jnp.zeros((8, LANES), jnp.float32)
        for i in range(cap_tiles):
            key = tiles[i][-1]
            least = jnp.min(key, axis=1, keepdims=True)
            most = jnp.max(jnp.where(key < none, key, -1.0), axis=1, keepdims=True)
            bounds = jnp.where(lane == i, jnp.floor(least * (1.0 / radial)), bounds)
            bounds = jnp.where(lane == HALF + i, jnp.floor(most * (1.0 / radial)), bounds)
        row = h * 8 * slots.rows
        out_ref[pl.ds(row, 8, stride=slots.rows), :] = bounds
        for i in range(cap_tiles):
            begin = row + slots.place(i // step) + fields * (i % step)
            for f in range(fields):
                out_ref[pl.ds(begin + f, 8, stride=slots.rows), :] = tiles[i][f]

    stores = []
    for h in range(seg_count // 8):
        group(h)
        for g in range(8 * h, 8 * h + 8):
            store = pltpu.make_async_copy(
                out_ref.at[g * slots.rows : (g + 1) * slots.rows, :], sends_hbm.at[g], out_sems.at[g]
            )
            store.start()
            stores.append(store)
    for store in stores:
        store.wait()


def base_kernel(state_ref, kappa_ref, out_ref, edge_ref):
    components, azim, radial = state_ref.shape
    lane = lax.broadcasted_iota(jnp.int32, (azim, radial), 1)
    sub = lax.broadcasted_iota(jnp.int32, (8, radial), 0)
    first = lane[:1] == 0
    last = lane[:1] == radial - 1
    pick = lax.broadcasted_iota(jnp.int32, (8, radial), 1)
    pick = ((sub == 2) & (pick == 0)) | ((sub == 3) & (pick == radial - 1))
    pick = jnp.where(pick, 1.0, 0.0).astype(jnp.bfloat16)
    none = jnp.zeros((1, radial), jnp.float32)

    def component(v, carry):
        q = state_ref[v]
        both = jnp.concatenate([q[1:], none], axis=0) + jnp.concatenate([none, q[:-1]], axis=0)
        column = both + 4.0 * q
        side = jnp.where(lane == radial - 1, 0.0, pltpu.roll(column, radial - 1, 1)) + jnp.where(
            lane == 0, 0.0, pltpu.roll(column, 1, 1)
        )
        total = side + (4.0 * both - 20.0 * q)
        out_ref[v] = q + time_step * (kappa_ref[...] * total / 6.0)

        def along(row):
            right = jnp.where(last, 0.0, pltpu.roll(row, radial - 1, 1))
            left = jnp.where(first, 0.0, pltpu.roll(row, 1, 1))
            return 4.0 * row + right + left

        top, bottom = q[:1], q[-1:]
        high, low = halves(column)
        turned = sum(
            lax.dot_general(pick, x, (TURNED, ((), ())), preferred_element_type=jnp.float32) for x in (high, low)
        )
        edge_ref[v] = jnp.where(
            sub == 0,
            along(top),
            jnp.where(sub == 1, along(bottom), jnp.where(sub == 4, top, jnp.where(sub == 5, bottom, turned))),
        )
        return carry

    lax.fori_loop(0, components, component, 0)


def by_least(slots, live, keys):
    columns = keys.T
    count, rows = keys.shape[0], slots.cap_tiles
    deep = -(-rows // 8) * 8
    length = -(-count * rows // LANES) * LANES
    slot = lax.broadcasted_iota(jnp.int32, keys.shape, 0)
    row = lax.broadcasted_iota(jnp.int32, keys.shape, 1)
    keys = (jnp.where(live, keys, 600.0) * (HALF * count)) + (slot * HALF + row).astype(jnp.float32)
    turned = keys.T
    places = []
    for s in range(count):
        fewer = jnp.zeros((deep, LANES), jnp.float32)
        for other in range(count):
            column = turned[:deep, other : other + 1]
            fewer += jnp.where(column < keys[s : s + 1, :], 1.0, 0.0)
        if deep > rows:
            extra = sum(
                jnp.where(turned[rows:deep, other : other + 1] < keys[s : s + 1, :], 1.0, 0.0)
                for other in range(count)
            )
            places.append(jnp.sum(fewer, axis=0, keepdims=True) - jnp.sum(extra, axis=0, keepdims=True))
        else:
            places.append(jnp.sum(fewer, axis=0, keepdims=True))
    places = jnp.concatenate(places, axis=0).T
    spot = lax.broadcasted_iota(jnp.int32, (deep, length), 1).astype(jnp.float32)
    name = lax.broadcasted_iota(jnp.int32, (deep, length), 0).astype(jnp.float32)
    tables = [jnp.zeros((deep, length), jnp.float32) for k in range(3)]
    for s in range(count):
        here = (places[:deep, s : s + 1] == spot) & (name < rows)
        values = (name + float(s * HALF), columns[:deep, s : s + 1], columns[HALF : HALF + deep, s : s + 1])
        tables = [table + jnp.where(here, value, 0.0) for table, value in zip(tables, values)]
    return [jnp.sum(table, axis=0, keepdims=True) for table in tables]


def by_window(step, count, least, most):
    length = least.shape[1]
    spot = lax.broadcasted_iota(jnp.int32, (1, length), 1)
    far = most
    for q in range(1, step):
        far = jnp.maximum(far, jnp.where(spot + q < count, pltpu.roll(most, length - q, 1), -1.0))
    start = jnp.floor(least * 0.125)
    windows = jnp.floor((far - 8.0 * start) * (1.0 / WINDOW)) + 1.0
    windows = jnp.where((spot % step == 0) & (spot < count), windows, 0.0)
    row = lax.broadcasted_iota(jnp.int32, (length, length), 0)
    earlier = jnp.where(row < lax.broadcasted_iota(jnp.int32, (length, length), 1), 1.0, 0.0).astype(jnp.bfloat16)
    sub = lax.broadcasted_iota(jnp.int32, (8, length), 0)

    def dot(x, y):
        return lax.dot_general(x.astype(jnp.bfloat16), y, (PLAIN, ((), ())), preferred_element_type=jnp.float32)

    before = dot(jnp.where(sub == 0, windows, 0.0), earlier)[:1]
    columns = jnp.where(sub == 0, before, jnp.where(sub == 1, before + windows, 0.0)).T
    items = work_length(length // step)
    item = lax.broadcasted_iota(jnp.int32, (length, items), 1).astype(jnp.float32)
    here = (columns[:, 0:1] <= item) & (item < columns[:, 1:2])
    here = jnp.where(here, 1.0, 0.0).astype(jnp.bfloat16)
    high = jnp.floor(before * (1.0 / 256))
    chunk = (spot // step).astype(jnp.float32)
    found = dot(
        jnp.where(
            sub == 0,
            chunk,
            jnp.where(sub == 1, start, jnp.where(sub == 2, high, jnp.where(sub == 3, before - 256.0 * high, 0.0))),
        ),
        here,
    )
    first = 8.0 * found[1:2] + WINDOW * (item[:1] - (256.0 * found[2:3] + found[3:4]))
    total = jnp.sum(windows).astype(jnp.int32)
    return found[0:1], first, total


def work_length(chunks):
    return -(-(chunks * (256 // WINDOW + 1) + UNROLL) // LANES) * LANES


def add_chunks(slots, own, own_only, got_ref, sum_ref, list_ref, task_ref, order_ref, work_ref, sems):
    seg_count = got_ref.shape[0]
    components, _, radial = sum_ref.shape
    azim = sum_ref.shape[1] - WINDOW
    fields, step = slots.fields, slots.step
    width = step * LANES
    count = -(-seg_count // 8) * 8
    bounds = [got_ref[s, 0:1, :] for s in range(seg_count)]
    if count > seg_count:
        bounds.append(jnp.full((count - seg_count, LANES), -1.0, jnp.float32))
    bounds = jnp.concatenate(bounds, axis=0)
    most = pltpu.roll(bounds, LANES - HALF, 1)
    live = (most >= 0) & (lax.broadcasted_iota(jnp.int32, (count, LANES), 1) < slots.cap_tiles)
    if not own_only:
        live = live & (lax.broadcasted_iota(jnp.int32, (count, LANES), 0) != own)
    total_rows = jnp.sum(jnp.where(live, 1.0, 0.0)).astype(jnp.int32)
    order, least, most = by_least(slots, live, bounds)
    list_ref[0:1, :] = order.astype(jnp.int32)
    chunk, first, total = by_window(step, total_rows, least, most)
    task_ref[0:1, :] = chunk.astype(jnp.int32)
    unroll = OWN_UNROLL if own_only else UNROLL
    task = lax.broadcasted_iota(jnp.int32, first.shape, 1)
    task_ref[1:2, :] = jnp.where(task < total, first.astype(jnp.int32), azim)
    copies = [
        pltpu.make_async_copy(task_ref, work_ref, sems.at[0]),
        pltpu.make_async_copy(list_ref, order_ref, sems.at[1]),
    ]
    for copy in copies:
        copy.start()
    cells = lax.broadcasted_iota(jnp.int32, (radial, width), 0).astype(jnp.float32).astype(jnp.bfloat16)
    near = lax.broadcasted_iota(jnp.int32, (WINDOW, width), 0).astype(jnp.float32).astype(jnp.bfloat16)
    lanes = lax.broadcasted_iota(jnp.int32, (1, width), 1)
    none = float(azim * radial)
    for copy in copies:
        copy.wait()

    def block(t):
        c = work_ref[0, t]
        start = pl.multiple_of(work_ref[1, t], 8)
        rows = []
        for q in range(step):
            name = order_ref[0, c * step + q]
            rows.append(got_ref[name // HALF, pl.ds(8 + fields * (name % HALF), fields), :])

        def field(k):
            return jnp.concatenate([x[k : k + 1] for x in rows], axis=1)

        ids = jnp.where(lanes < (total_rows - c * step) * LANES, field(components), none)
        a = jnp.floor(ids * (1.0 / radial))
        b = (ids - radial * a).astype(jnp.bfloat16)
        right = jnp.where(cells == b, jnp.bfloat16(1), jnp.bfloat16(0))
        in_a = near == (a - start.astype(jnp.float32)).astype(jnp.bfloat16)
        highs, lows = [], []
        for v in range(components):
            values = field(v)
            high = values.astype(jnp.bfloat16)
            low = (values - high.astype(jnp.float32)).astype(jnp.bfloat16)
            highs.append(jnp.where(in_a, high, jnp.bfloat16(0)))
            lows.append(jnp.where(in_a, low, jnp.bfloat16(0)))
        left = jnp.concatenate(highs + lows, axis=0)
        part = lax.dot_general(left, right, (TURNED, ((), ())), preferred_element_type=jnp.float32)
        part = part[: components * WINDOW] + part[components * WINDOW :]
        return start, part

    def several(t, carry):
        done = [block(t * unroll + u) for u in range(unroll)]
        for start, part in done:
            for v in range(components):
                sum_ref[v, pl.ds(start, WINDOW), :] += part[v * WINDOW : (v + 1) * WINDOW]
        return carry

    lax.fori_loop(0, (total + unroll - 1) // unroll, several, 0)


def own_kernel(slots, sends_hbm, sum_ref, held_ref, *work):
    own = lax.axis_index("segaz")
    load = pltpu.make_async_copy(sends_hbm.at[own], held_ref.at[0], work[-1])
    load.start()
    sum_ref[...] = jnp.zeros(sum_ref.shape, jnp.float32)
    load.wait()
    add_chunks(slots, own, True, held_ref, sum_ref, *work[:-1])


def rest_kernel(
    slots,
    map_ref, match_ref, got_ref, begun_ref, face_ref, edge_ref, near_ref, far_ref,
    sum_ref, joint_ref, before_ref, after_ref, side_ref,
    *work,
):
    seg_count = got_ref.shape[0]
    components, _, radial = sum_ref.shape
    azim = sum_ref.shape[1] - WINDOW
    sum_ref[...] = begun_ref[...]
    own = lax.axis_index("segaz")
    add_chunks(slots, own, False, got_ref, sum_ref, *work)

    partner = jnp.int32(0)
    target = match_ref[map_ref[own]]
    for h in range(seg_count):
        partner = jnp.where(map_ref[h] == target, h, partner)
    layer = lax.broadcasted_iota(jnp.int32, (JL, radial), 0)
    strength = jnp.zeros((JL, radial), jnp.float32)
    for l in range(JL):
        strength = jnp.where(layer == l, layer_weights[l], strength)
    for v in range(components):
        tile = got_ref[partner, slots.face + 8 * v : slots.face + 8 * v + 8, :]
        face = jnp.concatenate([tile[:JL], tile[JL:]], axis=1)
        joint_ref[v, 0:JL, :] = strength * (face - face_ref[v, 0:JL, :])
        joint_ref[v, JL:8, :] = jnp.zeros((8 - JL, radial), jnp.float32)

    near = halves(near_ref[...])
    far = halves(far_ref[...])
    inner = tuple(x[:, :radial] for x in far)
    ends = tuple(jnp.concatenate([x[:, :16], x[:, azim - 16 :]], axis=1) for x in near)
    rows, columns = [], []
    for v in range(components):
        cells_v = halves(sum_ref[v, 0:azim, :])
        edges = tuple(jnp.concatenate([x[:16], x[azim - 16 :]], axis=0) for x in cells_v)
        rows.append(product(ends, edges, PLAIN))
        columns.append(product(near, cells_v, TURNED))
    rows = product(jnp.concatenate(rows, axis=0), inner, PLAIN)
    columns = product(jnp.concatenate(columns, axis=0), far, PLAIN)
    sub = lax.broadcasted_iota(jnp.int32, (8, LANES), 0)
    lane = lax.broadcasted_iota(jnp.int32, (8, LANES), 1)
    half = LANES
    for v in range(components):
        row = rows[16 * v : 16 * v + 16]
        column = columns[16 * v : 16 * v + 16]
        edge = edge_ref[v]
        wide = lax.broadcasted_iota(jnp.int32, (8, radial), 0)
        after_ref[v, :, :radial] = jnp.where(wide == FW, edge[1:2], row[8:16])
        before_ref[v, :, :radial] = jnp.where(
            wide == FW - 1, edge[0:1], jnp.concatenate([row[FW:8], row[0:FW]], axis=0)
        )
        bottom, top = edge[5:6], edge[4:5]
        left_corner = jnp.where(lane[:1] == 0, bottom[:, :half], 0.0)
        right_corner = jnp.where(lane[:1] == 0, pltpu.roll(bottom[:, radial - half :], 1, 1), 0.0)
        after_ref[v, :, radial : radial + half] = jnp.where(
            sub == FW, left_corner, column[0:8, radial + half : radial + 2 * half]
        )
        after_ref[v, :, radial + half : radial + 2 * half] = jnp.where(
            sub == FW, right_corner, column[8:16, radial + half : radial + 2 * half]
        )
        left_corner = jnp.where(lane[:1] == half - 1, pltpu.roll(top[:, :half], half - 1, 1), 0.0)
        right_corner = jnp.where(lane[:1] == half - 1, top[:, radial - half :], 0.0)
        before_ref[v, :, radial : radial + half] = jnp.where(
            sub == FW, left_corner, column[0:8, radial : radial + half]
        )
        before_ref[v, :, radial + half : radial + 2 * half] = jnp.where(
            sub == FW, right_corner, column[8:16, radial : radial + half]
        )
        side_ref[v, 0:8, :] = jnp.where(wide == FW, edge[2:3], column[0:8, :radial])
        side_ref[v, 8:16, :] = jnp.where(wide == FW, edge[3:4], column[8:16, :radial])


def inner_kernel(sum_ref, base_ref, joint_ref, band_ref, out_ref):
    components, azim, radial = base_ref.shape
    band = halves(band_ref[...])

    def component(v, carry):
        across = product(sum_ref[v, 0:azim, :], band, PLAIN)
        both = product(band, across, PLAIN)
        out_ref[v] = base_ref[v] + time_step * both
        out_ref[v, 0:8, :] += time_step * joint_ref[v]
        return carry

    lax.fori_loop(0, components, component, 0)


def corner_kernel(side_ref, prior_ref, next_ref, left_ref, right_ref):
    radial = left_ref.shape[2]
    for out_ref, begin, corner in ((left_ref, 0, radial), (right_ref, 8, radial + LANES)):
        out_ref[:, :, :LANES] = (
            side_ref[:, begin : begin + 8, :LANES] + prior_ref[:, :, corner : corner + LANES]
        )
        out_ref[:, :, LANES:] = (
            side_ref[:, begin : begin + 8, LANES:] + next_ref[:, :, corner : corner + LANES]
        )


def final_kernel(inner_ref, kappa_ref, prior_ref, next_ref, left_ref, right_ref, pick_ref, out_ref):
    v = pl.program_id(0)
    azim, radial = kappa_ref.shape
    pick = pick_ref[...].astype(jnp.bfloat16)
    sub = lax.broadcasted_iota(jnp.int32, (8, radial), 0)
    parts = halves(jnp.concatenate([left_ref[v], right_ref[v]], axis=0))
    sides = sum(
        lax.dot_general(x, pick, (((0,), (0,)), ((), ())), preferred_element_type=jnp.float32) for x in parts
    )
    kappa = kappa_ref[...]
    out_ref[0] = inner_ref[v] + time_step * (sides[:, :radial] + kappa * sides[:, radial:] / 6.0)
    prior = prior_ref[v, :, :radial]
    add = jnp.where(sub < FW, prior, 0.0) + jnp.where(sub == 0, kappa[0:8] * prior[FW : FW + 1] / 6.0, 0.0)
    out_ref[0, 0:8, :] += time_step * add
    nxt = next_ref[v, :, :radial]
    add = jnp.where(sub >= 8 - FW, nxt, 0.0) + jnp.where(
        sub == 7, kappa[azim - 8 : azim] * nxt[FW - 1 : FW] / 6.0, 0.0
    )
    out_ref[0, azim - 8 : azim, :] += time_step * add


def call(kernel, outs, ins, scratch=(), cost=None, to="vmem", room=48):
    spaces = {"smem": pltpu.SMEM, "vmem": pltpu.VMEM, "hbm": pltpu.HBM, "any": pl.ANY}

    def spec(where):
        if isinstance(where, str):
            return pl.BlockSpec(memory_space=spaces[where])
        return pl.BlockSpec(where, lambda i: (0,) * len(where))

    return pl.pallas_call(
        kernel,
        grid=(1,),
        out_shape=[jax.ShapeDtypeStruct(shape, jnp.float32) for shape in outs],
        in_specs=[spec(where) for where in ins],
        out_specs=[spec(to)] * len(outs),
        scratch_shapes=list(scratch),
        cost_estimate=None
        if cost is None
        else pl.CostEstimate(flops=cost, bytes_accessed=cost // 1000, transcendentals=0),
        compiler_params=pltpu.CompilerParams(vmem_limit_bytes=room << 20),
    )


def shifted(strip, axis, way):
    count = lax.axis_size(axis)
    pairs = [(i, i + 1) if way > 0 else (i + 1, i) for i in range(count - 1)]
    return lax.ppermute(strip, axis, pairs)


def local(state, kappa, drop_src, drop_cell, drop_count, part_map, match_block):
    components, azim, radial = state.shape
    row_count = drop_src.shape[1]
    seg_count = lax.axis_size("segaz")
    capacity = 5 * row_count // (4 * seg_count)
    cap_tiles = capacity // LANES
    slots = Slots(components, cap_tiles, STEP if cap_tiles % STEP == 0 else 2)
    face = (components, 8, radial)
    whole = state.shape
    sums = (components, azim + WINDOW, radial)
    strip = (components, 8, 2 * radial)
    sides = (components, 8, radial)
    (sends,) = call(
        functools.partial(pack_kernel, slots, azim),
        [(seg_count, slots.rows, LANES)],
        ["hbm"] * 4,
        [
            pltpu.SMEM(drop_count.shape[:1] + (seg_count,), jnp.int32),
            pltpu.VMEM(drop_src.shape, jnp.float32),
            pltpu.VMEM((row_count // LANES, LANES), jnp.int32),
            pltpu.VMEM(face, jnp.float32),
            pltpu.VMEM((seg_count * slots.rows, LANES), jnp.float32),
            pltpu.VMEM((seg_count // 8, cap_tiles, 64, LANES), jnp.float32),
            pltpu.SemaphoreType.DMA((3 + PIECES,)),
            pltpu.SemaphoreType.DMA((seg_count,)),
        ],
        to="hbm",
        room=62,
    )(drop_count, drop_src, drop_cell.reshape(-1, LANES), state)
    got = lax.all_to_all(sends, "segaz", split_axis=0, concat_axis=0, tiled=True)

    def work(count):
        length = -(-(-(-count // 8) * 8) * cap_tiles // LANES) * LANES
        return [
            pltpu.VMEM((8, length), jnp.int32),
            pltpu.VMEM((8, work_length(length // slots.step)), jnp.int32),
            pltpu.SMEM((8, length), jnp.int32),
            pltpu.SMEM((8, work_length(length // slots.step)), jnp.int32),
            pltpu.SemaphoreType.DMA((2,)),
        ]

    (begun,) = call(
        functools.partial(own_kernel, slots),
        [sums],
        ["hbm"],
        [pltpu.VMEM((1, slots.rows, LANES), jnp.float32)] + work(1) + [pltpu.SemaphoreType.DMA(())],
        cost=1 << 23,
    )(sends)
    still, edge = call(base_kernel, [whole, face], ["vmem", "vmem"], cost=1 << 22)(state, kappa)
    near = jnp.asarray(taps(edge_targets(azim), azim))
    far = jnp.asarray(taps(extended_targets(azim), azim).T)
    band = jnp.asarray(taps(list(range(azim)), azim))
    source, joint, before, after, side = call(
        functools.partial(rest_kernel, slots),
        [sums, face, strip, strip, (components, 16, radial)],
        ["smem", "smem", "vmem", "vmem", face, "vmem", "vmem", "vmem"],
        work(seg_count),
    )(part_map, match_block, got, begun, state, edge, near, far)
    prior = shifted(after, "segaz", 1)
    nxt = shifted(before, "segaz", -1)
    (inner,) = call(inner_kernel, [whole], ["vmem"] * 4, cost=1 << 22)(source, still, joint, band)
    to_left, to_right = call(corner_kernel, [sides, sides], ["vmem"] * 3)(side, prior, nxt)
    left = shifted(to_right, "rad", 1)
    right = shifted(to_left, "rad", -1)
    pick = jnp.asarray(pick_columns(radial))
    return pl.pallas_call(
        final_kernel,
        grid=(components,),
        out_shape=jax.ShapeDtypeStruct(whole, jnp.float32),
        in_specs=[pl.BlockSpec(memory_space=pltpu.VMEM)] * 7,
        out_specs=pl.BlockSpec((1, azim, radial), lambda v: (v, 0, 0)),
        compiler_params=pltpu.CompilerParams(vmem_limit_bytes=48 << 20),
    )(inner, kappa, prior, nxt, left, right, pick)


def solution(mesh):
    return jax.shard_map(
        local,
        mesh=mesh,
        in_specs=(
            P(None, "segaz", "rad"),
            P("segaz", "rad"),
            P(None, ("segaz", "rad")),
            P(("segaz", "rad")),
            P(("segaz", "rad"), None),
            P(),
            P(),
        ),
        out_specs=P(None, "segaz", "rad"),
        check_vma=False,
    )
```

```python
import functools

import jax
import jax.numpy as jnp
import numpy as np
from jax import lax
from jax.experimental import pallas as pl
from jax.experimental.pallas import tpu as pltpu
from jax.sharding import PartitionSpec as P

FW = 4
JL = 4
LANES = 128
WINDOW = 48
ROUNDS = 6
UNROLL = 16
OWN_UNROLL = 5
STEP = 4
PIECES = 4
HALF = 64

time_step = 0.25
layer_weights = (1.0, 0.6, 0.35, 0.2)


def filter_weights(half_width):
    offsets = np.arange(-half_width, half_width + 1).astype(np.float32)
    bell_curve = np.exp(-offsets * offsets / np.float32(8.0))
    return bell_curve / np.sum(bell_curve)


def taps(targets, length):
    weights = filter_weights(FW)
    table = np.zeros((len(targets), length), np.float32)
    for i, cell in enumerate(targets):
        if cell is not None:
            for k in range(-FW, FW + 1):
                if 0 <= cell + k < length:
                    table[i, cell + k] = weights[k + FW]
    return table


def edge_targets(length):
    gap = [None] * (8 - FW)
    return list(range(-FW, 0)) + gap + list(range(length, length + FW)) + gap


def extended_targets(length):
    gap = [None] * (LANES - FW)
    return list(range(length)) + gap + list(range(-FW, 0)) + list(range(length, length + FW)) + gap


def pick_columns(radial):
    table = np.zeros((16, 2 * radial), np.float32)
    for k in range(FW):
        table[k, k] = 1.0
        table[8 + k, radial - FW + k] = 1.0
    table[FW, radial] = 1.0
    table[8 + FW, 2 * radial - 1] = 1.0
    return table


def halves(x):
    high = x.astype(jnp.bfloat16)
    return high, (x - high.astype(jnp.float32)).astype(jnp.bfloat16)


def product(x, y, dims):
    xh, xl = halves(x) if not isinstance(x, tuple) else x
    yh, yl = halves(y) if not isinstance(y, tuple) else y

    def dot(p, q):
        return lax.dot_general(p, q, (dims, ((), ())), preferred_element_type=jnp.float32)

    both = dot(jnp.concatenate([xh, xl], axis=0), yh)
    count = xh.shape[0]
    return both[:count] + (both[count:] + dot(xh, yl))


PLAIN = ((1,), (0,))
TURNED = ((1,), (1,))


def comparators(count):
    size = 1 << (count - 1).bit_length()
    pairs = []
    p = 1
    while p < size:
        k = p
        while k >= 1:
            for j in range(k % p, size - k, 2 * k):
                for i in range(min(k, size - j - k)):
                    if (i + j) // (2 * p) == (i + j + k) // (2 * p) and i + j + k < count:
                        pairs.append((i + j, i + j + k))
            k //= 2
        p *= 2
    return pairs


def touch_up(count):
    return [
        (i, i + d) for d in (2, 1) for odd in (0, 1) for i in range(count - d) if i // d % 2 == odd
    ]


def sort_rows(tiles, pairs):
    for low, high in pairs:
        swap = tiles[high][-1] < tiles[low][-1]
        first = [jnp.where(swap, y, x) for x, y in zip(tiles[low], tiles[high])]
        second = [jnp.where(swap, x, y) for x, y in zip(tiles[low], tiles[high])]
        tiles[low], tiles[high] = first, second
    return tiles


class Slots:
    def __init__(self, components, cap_tiles, step):
        self.fields = components + 1
        self.cap_tiles, self.step = cap_tiles, step
        self.chunks = cap_tiles // step
        self.chunk_rows = self.fields * step
        self.face = -(-(8 + self.chunks * self.chunk_rows) // 8) * 8
        self.rows = self.face + 8 * components

    def place(self, j):
        return 8 + j * self.chunk_rows


def pack_kernel(
    slots, azim,
    count_hbm, src_hbm, cell_hbm, state_hbm, *refs,
):
    sends_hbm, count_ref, src_ref, cell_ref, face_ref, out_ref, held_ref, in_sems, out_sems = refs
    cap_tiles, step = slots.cap_tiles, slots.step
    components, row_count = src_ref.shape
    fields = components + 1
    tile_count = cell_ref.shape[0]
    radial = face_ref.shape[2]
    seg_count = sends_hbm.shape[0]
    piece = row_count // PIECES
    loads = [
        pltpu.make_async_copy(count_hbm, count_ref, in_sems.at[0]),
        pltpu.make_async_copy(state_hbm.at[:, 0:8, :], face_ref, in_sems.at[1]),
        pltpu.make_async_copy(cell_hbm, cell_ref, in_sems.at[2]),
    ] + [
        pltpu.make_async_copy(
            src_hbm.at[:, k * piece : (k + 1) * piece], src_ref.at[:, k * piece : (k + 1) * piece], in_sems.at[3 + k]
        )
        for k in range(PIECES)
    ]
    for load in loads:
        load.start()
    for load in loads:
        load.wait()
    lane = lax.broadcasted_iota(jnp.int32, (8, LANES), 1)
    sub = lax.broadcasted_iota(jnp.int32, (8, LANES), 0)
    none = float(azim * radial)

    def slot(g, begin):
        count = count_ref[0, g]
        first = begin // LANES
        shift = begin % LANES
        turn = (LANES - shift) % LANES

        def rolled(i):
            t = jnp.minimum(first + i, tile_count - 1)
            src = src_ref[:, pl.ds(pl.multiple_of(t * LANES, LANES), LANES)]
            cell = cell_ref[pl.ds(t, 1), :].astype(jnp.float32)
            both = jnp.concatenate([src, cell, jnp.zeros((8 - fields, LANES), jnp.float32)], axis=0)
            return pltpu.roll(both, turn, 1)

        row = g * slots.rows + slots.face
        for v in range(components):
            for half in range(2):
                out_ref[pl.ds(row + 8 * v + 4 * half, JL), :] = face_ref[
                    v, 0:JL, half * LANES : (half + 1) * LANES
                ]
        head = rolled(0)
        for i in range(cap_tiles):
            tail = rolled(i + 1)
            rows = jnp.where(lane < LANES - shift, head, tail)
            dead = (sub == components) & (lane >= count - i * LANES)
            rows = jnp.where(dead, none, rows)
            held_ref[g // 8, i, pl.ds(g % 8, 8, stride=8), :] = rows
            head = tail
        return begin + count

    lax.fori_loop(0, seg_count, slot, jnp.int32(0))

    def group(h):
        tiles = [
            [held_ref[h, i, 8 * f : 8 * f + 8, :] for f in range(fields)] for i in range(cap_tiles)
        ]
        tiles = sort_rows(tiles, comparators(cap_tiles))
        for again in range(ROUNDS):
            tiles = [[pltpu.roll(x, (37 * i) % LANES, 1) for x in tiles[i]] for i in range(cap_tiles)]
            tiles = sort_rows(tiles, touch_up(cap_tiles))
        bounds = jnp.zeros((8, LANES), jnp.float32)
        for i in range(cap_tiles):
            key = tiles[i][-1]
            least = jnp.min(key, axis=1, keepdims=True)
            most = jnp.max(jnp.where(key < none, key, -1.0), axis=1, keepdims=True)
            bounds = jnp.where(lane == i, jnp.floor(least * (1.0 / radial)), bounds)
            bounds = jnp.where(lane == HALF + i, jnp.floor(most * (1.0 / radial)), bounds)
        row = h * 8 * slots.rows
        out_ref[pl.ds(row, 8, stride=slots.rows), :] = bounds
        for i in range(cap_tiles):
            begin = row + slots.place(i // step) + fields * (i % step)
            for f in range(fields):
                out_ref[pl.ds(begin + f, 8, stride=slots.rows), :] = tiles[i][f]

    stores = []
    for h in range(seg_count // 8):
        group(h)
        for g in range(8 * h, 8 * h + 8):
            store = pltpu.make_async_copy(
                out_ref.at[g * slots.rows : (g + 1) * slots.rows, :], sends_hbm.at[g], out_sems.at[g]
            )
            store.start()
            stores.append(store)
    for store in stores:
        store.wait()


def base_kernel(state_ref, kappa_ref, out_ref, edge_ref):
    components, azim, radial = state_ref.shape
    lane = lax.broadcasted_iota(jnp.int32, (azim, radial), 1)
    sub = lax.broadcasted_iota(jnp.int32, (8, radial), 0)
    first = lane[:1] == 0
    last = lane[:1] == radial - 1
    pick = lax.broadcasted_iota(jnp.int32, (8, radial), 1)
    pick = ((sub == 2) & (pick == 0)) | ((sub == 3) & (pick == radial - 1))
    pick = jnp.where(pick, 1.0, 0.0).astype(jnp.bfloat16)
    none = jnp.zeros((1, radial), jnp.float32)

    def component(v, carry):
        q = state_ref[v]
        both = jnp.concatenate([q[1:], none], axis=0) + jnp.concatenate([none, q[:-1]], axis=0)
        column = both + 4.0 * q
        side = jnp.where(lane == radial - 1, 0.0, pltpu.roll(column, radial - 1, 1)) + jnp.where(
            lane == 0, 0.0, pltpu.roll(column, 1, 1)
        )
        total = side + (4.0 * both - 20.0 * q)
        out_ref[v] = q + (time_step / 6.0) * (kappa_ref[...] * total)

        def along(row):
            right = jnp.where(last, 0.0, pltpu.roll(row, radial - 1, 1))
            left = jnp.where(first, 0.0, pltpu.roll(row, 1, 1))
            return 4.0 * row + right + left

        top, bottom = q[:1], q[-1:]
        high, low = halves(column)
        turned = sum(
            lax.dot_general(pick, x, (TURNED, ((), ())), preferred_element_type=jnp.float32) for x in (high, low)
        )
        edge_ref[v] = jnp.where(
            sub == 0,
            along(top),
            jnp.where(sub == 1, along(bottom), jnp.where(sub == 4, top, jnp.where(sub == 5, bottom, turned))),
        )
        return carry

    lax.fori_loop(0, components, component, 0)


def by_least(slots, live, keys):
    columns = keys.T
    count, rows = keys.shape[0], slots.cap_tiles
    deep = -(-rows // 8) * 8
    length = -(-count * rows // LANES) * LANES
    slot = lax.broadcasted_iota(jnp.int32, keys.shape, 0)
    row = lax.broadcasted_iota(jnp.int32, keys.shape, 1)
    keys = (jnp.where(live, keys, 600.0) * (HALF * count)) + (slot * HALF + row).astype(jnp.float32)
    turned = keys.T
    places = []
    for s in range(count):
        fewer = jnp.zeros((deep, LANES), jnp.float32)
        for other in range(count):
            column = turned[:deep, other : other + 1]
            fewer += jnp.where(column < keys[s : s + 1, :], 1.0, 0.0)
        if deep > rows:
            extra = sum(
                jnp.where(turned[rows:deep, other : other + 1] < keys[s : s + 1, :], 1.0, 0.0)
                for other in range(count)
            )
            places.append(jnp.sum(fewer, axis=0, keepdims=True) - jnp.sum(extra, axis=0, keepdims=True))
        else:
            places.append(jnp.sum(fewer, axis=0, keepdims=True))
    places = jnp.concatenate(places, axis=0).T
    spot = lax.broadcasted_iota(jnp.int32, (deep, length), 1).astype(jnp.float32)
    name = lax.broadcasted_iota(jnp.int32, (deep, length), 0).astype(jnp.float32)
    tables = [jnp.zeros((deep, length), jnp.float32) for k in range(3)]
    for s in range(count):
        here = (places[:deep, s : s + 1] == spot) & (name < rows)
        values = (name + float(s * HALF), columns[:deep, s : s + 1], columns[HALF : HALF + deep, s : s + 1])
        tables = [table + jnp.where(here, value, 0.0) for table, value in zip(tables, values)]
    return [jnp.sum(table, axis=0, keepdims=True) for table in tables]


def by_window(step, count, least, most):
    length = least.shape[1]
    spot = lax.broadcasted_iota(jnp.int32, (1, length), 1)
    far = most
    for q in range(1, step):
        far = jnp.maximum(far, jnp.where(spot + q < count, pltpu.roll(most, length - q, 1), -1.0))
    start = jnp.floor(least * 0.125)
    windows = jnp.floor((far - 8.0 * start) * (1.0 / WINDOW)) + 1.0
    windows = jnp.where((spot % step == 0) & (spot < count), windows, 0.0)
    row = lax.broadcasted_iota(jnp.int32, (length, length), 0)
    earlier = jnp.where(row < lax.broadcasted_iota(jnp.int32, (length, length), 1), 1.0, 0.0).astype(jnp.bfloat16)
    sub = lax.broadcasted_iota(jnp.int32, (8, length), 0)

    def dot(x, y):
        return lax.dot_general(x.astype(jnp.bfloat16), y, (PLAIN, ((), ())), preferred_element_type=jnp.float32)

    before = dot(jnp.where(sub == 0, windows, 0.0), earlier)[:1]
    columns = jnp.where(sub == 0, before, jnp.where(sub == 1, before + windows, 0.0)).T
    items = work_length(length // step)
    item = lax.broadcasted_iota(jnp.int32, (length, items), 1).astype(jnp.float32)
    here = (columns[:, 0:1] <= item) & (item < columns[:, 1:2])
    here = jnp.where(here, 1.0, 0.0).astype(jnp.bfloat16)
    high = jnp.floor(before * (1.0 / 256))
    chunk = (spot // step).astype(jnp.float32)
    found = dot(
        jnp.where(
            sub == 0,
            chunk,
            jnp.where(sub == 1, start, jnp.where(sub == 2, high, jnp.where(sub == 3, before - 256.0 * high, 0.0))),
        ),
        here,
    )
    first = 8.0 * found[1:2] + WINDOW * (item[:1] - (256.0 * found[2:3] + found[3:4]))
    total = jnp.sum(windows).astype(jnp.int32)
    return found[0:1], first, total


def work_length(chunks):
    return -(-(chunks * (256 // WINDOW + 1) + UNROLL) // LANES) * LANES


def add_chunks(slots, own, own_only, got_ref, sum_ref, list_ref, task_ref, order_ref, work_ref, sems):
    seg_count = got_ref.shape[0]
    components, _, radial = sum_ref.shape
    azim = sum_ref.shape[1] - WINDOW
    fields, step = slots.fields, slots.step
    width = step * LANES
    count = -(-seg_count // 8) * 8
    bounds = [got_ref[s, 0:1, :] for s in range(seg_count)]
    if count > seg_count:
        bounds.append(jnp.full((count - seg_count, LANES), -1.0, jnp.float32))
    bounds = jnp.concatenate(bounds, axis=0)
    most = pltpu.roll(bounds, LANES - HALF, 1)
    live = (most >= 0) & (lax.broadcasted_iota(jnp.int32, (count, LANES), 1) < slots.cap_tiles)
    if not own_only:
        live = live & (lax.broadcasted_iota(jnp.int32, (count, LANES), 0) != own)
    total_rows = jnp.sum(jnp.where(live, 1.0, 0.0)).astype(jnp.int32)
    order, least, most = by_least(slots, live, bounds)
    list_ref[0:1, :] = order.astype(jnp.int32)
    chunk, first, total = by_window(step, total_rows, least, most)
    task_ref[0:1, :] = chunk.astype(jnp.int32)
    unroll = OWN_UNROLL if own_only else UNROLL
    task = lax.broadcasted_iota(jnp.int32, first.shape, 1)
    task_ref[1:2, :] = jnp.where(task < total, first.astype(jnp.int32), azim)
    copies = [
        pltpu.make_async_copy(task_ref, work_ref, sems.at[0]),
        pltpu.make_async_copy(list_ref, order_ref, sems.at[1]),
    ]
    for copy in copies:
        copy.start()
    cells = lax.broadcasted_iota(jnp.int32, (radial, width), 0).astype(jnp.float32).astype(jnp.bfloat16)
    near = lax.broadcasted_iota(jnp.int32, (WINDOW, width), 0).astype(jnp.float32).astype(jnp.bfloat16)
    lanes = lax.broadcasted_iota(jnp.int32, (1, width), 1)
    none = float(azim * radial)
    for copy in copies:
        copy.wait()

    def block(t):
        c = work_ref[0, t]
        start = pl.multiple_of(work_ref[1, t], 8)
        rows = []
        for q in range(step):
            name = order_ref[0, c * step + q]
            rows.append(got_ref[name // HALF, pl.ds(8 + fields * (name % HALF), fields), :])

        def field(k):
            return jnp.concatenate([x[k : k + 1] for x in rows], axis=1)

        ids = jnp.where(lanes < (total_rows - c * step) * LANES, field(components), none)
        a = jnp.floor(ids * (1.0 / radial))
        b = (ids - radial * a).astype(jnp.bfloat16)
        right = jnp.where(cells == b, jnp.bfloat16(1), jnp.bfloat16(0))
        in_a = near == (a - start.astype(jnp.float32)).astype(jnp.bfloat16)
        highs, lows = [], []
        for v in range(components):
            values = field(v)
            high = values.astype(jnp.bfloat16)
            low = (values - high.astype(jnp.float32)).astype(jnp.bfloat16)
            highs.append(jnp.where(in_a, high, jnp.bfloat16(0)))
            lows.append(jnp.where(in_a, low, jnp.bfloat16(0)))
        left = jnp.concatenate(highs + lows, axis=0)
        part = lax.dot_general(left, right, (TURNED, ((), ())), preferred_element_type=jnp.float32)
        part = part[: components * WINDOW] + part[components * WINDOW :]
        return start, part

    def several(t, carry):
        done = [block(t * unroll + u) for u in range(unroll)]
        for start, part in done:
            for v in range(components):
                sum_ref[v, pl.ds(start, WINDOW), :] += part[v * WINDOW : (v + 1) * WINDOW]
        return carry

    lax.fori_loop(0, (total + unroll - 1) // unroll, several, 0)


def own_kernel(slots, sends_hbm, sum_ref, held_ref, *work):
    own = lax.axis_index("segaz")
    load = pltpu.make_async_copy(sends_hbm.at[own], held_ref.at[0], work[-1])
    load.start()
    sum_ref[...] = jnp.zeros(sum_ref.shape, jnp.float32)
    load.wait()
    add_chunks(slots, own, True, held_ref, sum_ref, *work[:-1])


def rest_kernel(
    slots,
    map_ref, match_ref, got_ref, begun_ref, face_ref, edge_ref, near_ref, far_ref,
    sum_ref, joint_ref, before_ref, after_ref, side_ref,
    *work,
):
    seg_count = got_ref.shape[0]
    components, _, radial = sum_ref.shape
    azim = sum_ref.shape[1] - WINDOW
    sum_ref[...] = begun_ref[...]
    own = lax.axis_index("segaz")
    add_chunks(slots, own, False, got_ref, sum_ref, *work)

    partner = jnp.int32(0)
    target = match_ref[map_ref[own]]
    for h in range(seg_count):
        partner = jnp.where(map_ref[h] == target, h, partner)
    layer = lax.broadcasted_iota(jnp.int32, (JL, radial), 0)
    strength = jnp.zeros((JL, radial), jnp.float32)
    for l in range(JL):
        strength = jnp.where(layer == l, layer_weights[l], strength)
    for v in range(components):
        tile = got_ref[partner, slots.face + 8 * v : slots.face + 8 * v + 8, :]
        face = jnp.concatenate([tile[:JL], tile[JL:]], axis=1)
        joint_ref[v, 0:JL, :] = strength * (face - face_ref[v, 0:JL, :])
        joint_ref[v, JL:8, :] = jnp.zeros((8 - JL, radial), jnp.float32)

    near = halves(near_ref[...])
    far = halves(far_ref[...])
    inner = tuple(x[:, :radial] for x in far)
    ends = tuple(jnp.concatenate([x[:, :16], x[:, azim - 16 :]], axis=1) for x in near)
    rows, columns = [], []
    for v in range(components):
        cells_v = halves(sum_ref[v, 0:azim, :])
        edges = tuple(jnp.concatenate([x[:16], x[azim - 16 :]], axis=0) for x in cells_v)
        rows.append(product(ends, edges, PLAIN))
        columns.append(product(near, cells_v, TURNED))
    rows = product(jnp.concatenate(rows, axis=0), inner, PLAIN)
    columns = product(jnp.concatenate(columns, axis=0), far, PLAIN)
    sub = lax.broadcasted_iota(jnp.int32, (8, LANES), 0)
    lane = lax.broadcasted_iota(jnp.int32, (8, LANES), 1)
    half = LANES
    for v in range(components):
        row = rows[16 * v : 16 * v + 16]
        column = columns[16 * v : 16 * v + 16]
        edge = edge_ref[v]
        wide = lax.broadcasted_iota(jnp.int32, (8, radial), 0)
        after_ref[v, :, :radial] = jnp.where(wide == FW, edge[1:2], row[8:16])
        before_ref[v, :, :radial] = jnp.where(
            wide == FW - 1, edge[0:1], jnp.concatenate([row[FW:8], row[0:FW]], axis=0)
        )
        bottom, top = edge[5:6], edge[4:5]
        left_corner = jnp.where(lane[:1] == 0, bottom[:, :half], 0.0)
        right_corner = jnp.where(lane[:1] == 0, pltpu.roll(bottom[:, radial - half :], 1, 1), 0.0)
        after_ref[v, :, radial : radial + half] = jnp.where(
            sub == FW, left_corner, column[0:8, radial + half : radial + 2 * half]
        )
        after_ref[v, :, radial + half : radial + 2 * half] = jnp.where(
            sub == FW, right_corner, column[8:16, radial + half : radial + 2 * half]
        )
        left_corner = jnp.where(lane[:1] == half - 1, pltpu.roll(top[:, :half], half - 1, 1), 0.0)
        right_corner = jnp.where(lane[:1] == half - 1, top[:, radial - half :], 0.0)
        before_ref[v, :, radial : radial + half] = jnp.where(
            sub == FW, left_corner, column[0:8, radial : radial + half]
        )
        before_ref[v, :, radial + half : radial + 2 * half] = jnp.where(
            sub == FW, right_corner, column[8:16, radial : radial + half]
        )
        side_ref[v, 0:8, :] = jnp.where(wide == FW, edge[2:3], column[0:8, :radial])
        side_ref[v, 8:16, :] = jnp.where(wide == FW, edge[3:4], column[8:16, :radial])


def inner_kernel(sum_ref, base_ref, joint_ref, band_ref, out_ref):
    components, azim, radial = base_ref.shape
    band = halves(band_ref[...])

    def component(v, carry):
        across = product(sum_ref[v, 0:azim, :], band, PLAIN)
        both = product(band, across, PLAIN)
        out_ref[v] = base_ref[v] + time_step * both
        out_ref[v, 0:8, :] += time_step * joint_ref[v]
        return carry

    lax.fori_loop(0, components, component, 0)


def corner_kernel(side_ref, prior_ref, next_ref, left_ref, right_ref):
    radial = left_ref.shape[2]
    for out_ref, begin, corner in ((left_ref, 0, radial), (right_ref, 8, radial + LANES)):
        out_ref[:, :, :LANES] = (
            side_ref[:, begin : begin + 8, :LANES] + prior_ref[:, :, corner : corner + LANES]
        )
        out_ref[:, :, LANES:] = (
            side_ref[:, begin : begin + 8, LANES:] + next_ref[:, :, corner : corner + LANES]
        )


def final_kernel(inner_ref, kappa_ref, prior_ref, next_ref, left_ref, right_ref, pick_ref, out_hbm, out_ref, sems):
    components, azim, radial = out_ref.shape
    pick = pick_ref[...].astype(jnp.bfloat16)
    sub = lax.broadcasted_iota(jnp.int32, (8, radial), 0)
    stores = []
    for v in range(components):
        parts = halves(jnp.concatenate([left_ref[v], right_ref[v]], axis=0))
        sides = sum(
            lax.dot_general(x, pick, (((0,), (0,)), ((), ())), preferred_element_type=jnp.float32) for x in parts
        )
        kappa = kappa_ref[...]
        total = inner_ref[v] + time_step * sides[:, :radial] + (time_step / 6.0) * (kappa * sides[:, radial:])
        prior = prior_ref[v, :, :radial]
        add = jnp.where(sub < FW, prior, 0.0) + jnp.where(
            sub == 0, kappa[0:8] * (prior[FW : FW + 1] * (1.0 / 6.0)), 0.0
        )
        out_ref[v, 0:8, :] = total[0:8] + time_step * add
        out_ref[v, 8 : azim - 8, :] = total[8 : azim - 8]
        nxt = next_ref[v, :, :radial]
        add = jnp.where(sub >= 8 - FW, nxt, 0.0) + jnp.where(
            sub == 7, kappa[azim - 8 : azim] * (nxt[FW - 1 : FW] * (1.0 / 6.0)), 0.0
        )
        out_ref[v, azim - 8 : azim, :] = total[azim - 8 : azim] + time_step * add
        store = pltpu.make_async_copy(out_ref.at[v], out_hbm.at[v], sems.at[v])
        store.start()
        stores.append(store)
    for store in stores:
        store.wait()


def call(kernel, outs, ins, scratch=(), cost=None, to="vmem", room=48):
    spaces = {"smem": pltpu.SMEM, "vmem": pltpu.VMEM, "hbm": pltpu.HBM, "any": pl.ANY}

    def spec(where):
        if isinstance(where, str):
            return pl.BlockSpec(memory_space=spaces[where])
        return pl.BlockSpec(where, lambda i: (0,) * len(where))

    return pl.pallas_call(
        kernel,
        grid=(1,),
        out_shape=[jax.ShapeDtypeStruct(shape, jnp.float32) for shape in outs],
        in_specs=[spec(where) for where in ins],
        out_specs=[spec(to)] * len(outs),
        scratch_shapes=list(scratch),
        cost_estimate=None
        if cost is None
        else pl.CostEstimate(flops=cost, bytes_accessed=cost // 1000, transcendentals=0),
        compiler_params=pltpu.CompilerParams(vmem_limit_bytes=room << 20),
    )


def shifted(strip, axis, way):
    count = lax.axis_size(axis)
    pairs = [(i, i + 1) if way > 0 else (i + 1, i) for i in range(count - 1)]
    return lax.ppermute(strip, axis, pairs)


def local(state, kappa, drop_src, drop_cell, drop_count, part_map, match_block):
    components, azim, radial = state.shape
    row_count = drop_src.shape[1]
    seg_count = lax.axis_size("segaz")
    capacity = 5 * row_count // (4 * seg_count)
    cap_tiles = capacity // LANES
    slots = Slots(components, cap_tiles, STEP if cap_tiles % STEP == 0 else 2)
    face = (components, 8, radial)
    whole = state.shape
    sums = (components, azim + WINDOW, radial)
    strip = (components, 8, 2 * radial)
    sides = (components, 8, radial)
    (sends,) = call(
        functools.partial(pack_kernel, slots, azim),
        [(seg_count, slots.rows, LANES)],
        ["hbm"] * 4,
        [
            pltpu.SMEM(drop_count.shape[:1] + (seg_count,), jnp.int32),
            pltpu.VMEM(drop_src.shape, jnp.float32),
            pltpu.VMEM((row_count // LANES, LANES), jnp.int32),
            pltpu.VMEM(face, jnp.float32),
            pltpu.VMEM((seg_count * slots.rows, LANES), jnp.float32),
            pltpu.VMEM((seg_count // 8, cap_tiles, 64, LANES), jnp.float32),
            pltpu.SemaphoreType.DMA((3 + PIECES,)),
            pltpu.SemaphoreType.DMA((seg_count,)),
        ],
        to="hbm",
        room=62,
    )(drop_count, drop_src, drop_cell.reshape(-1, LANES), state)
    got = lax.all_to_all(sends, "segaz", split_axis=0, concat_axis=0, tiled=True)

    def work(count):
        length = -(-(-(-count // 8) * 8) * cap_tiles // LANES) * LANES
        return [
            pltpu.VMEM((8, length), jnp.int32),
            pltpu.VMEM((8, work_length(length // slots.step)), jnp.int32),
            pltpu.SMEM((8, length), jnp.int32),
            pltpu.SMEM((8, work_length(length // slots.step)), jnp.int32),
            pltpu.SemaphoreType.DMA((2,)),
        ]

    (begun,) = call(
        functools.partial(own_kernel, slots),
        [sums],
        ["hbm"],
        [pltpu.VMEM((1, slots.rows, LANES), jnp.float32)] + work(1) + [pltpu.SemaphoreType.DMA(())],
        cost=1 << 23,
    )(sends)
    still, edge = call(base_kernel, [whole, face], ["vmem", "vmem"], cost=1 << 22)(state, kappa)
    near = jnp.asarray(taps(edge_targets(azim), azim))
    far = jnp.asarray(taps(extended_targets(azim), azim).T)
    band = jnp.asarray(taps(list(range(azim)), azim))
    source, joint, before, after, side = call(
        functools.partial(rest_kernel, slots),
        [sums, face, strip, strip, (components, 16, radial)],
        ["smem", "smem", "vmem", "vmem", face, "vmem", "vmem", "vmem"],
        work(seg_count),
    )(part_map, match_block, got, begun, state, edge, near, far)
    prior = shifted(after, "segaz", 1)
    nxt = shifted(before, "segaz", -1)
    (inner,) = call(inner_kernel, [whole], ["vmem"] * 4, cost=1 << 22)(source, still, joint, band)
    to_left, to_right = call(corner_kernel, [sides, sides], ["vmem"] * 3)(side, prior, nxt)
    left = shifted(to_right, "rad", 1)
    right = shifted(to_left, "rad", -1)
    pick = jnp.asarray(pick_columns(radial))
    (result,) = call(
        final_kernel,
        [whole],
        ["vmem"] * 7,
        [pltpu.VMEM(whole, jnp.float32), pltpu.SemaphoreType.DMA((components,))],
        to="hbm",
    )(inner, kappa, prior, nxt, left, right, pick)
    return result


def solution(mesh):
    return jax.shard_map(
        local,
        mesh=mesh,
        in_specs=(
            P(None, "segaz", "rad"),
            P("segaz", "rad"),
            P(None, ("segaz", "rad")),
            P(("segaz", "rad")),
            P(("segaz", "rad"), None),
            P(),
            P(),
        ),
        out_specs=P(None, "segaz", "rad"),
        check_vma=False,
    )
```

```python
import functools

import jax
import jax.numpy as jnp
import numpy as np
from jax import lax
from jax.experimental import pallas as pl
from jax.experimental.pallas import tpu as pltpu
from jax.sharding import PartitionSpec as P

FW = 4
JL = 4
LANES = 128
WINDOW = 48
ROUNDS = 6
UNROLL = 16
OWN_UNROLL = 5
SPARE = 8
FEW = 4
STEP = 4
PIECES = 4
HALF = 64

time_step = 0.25
layer_weights = (1.0, 0.6, 0.35, 0.2)


def filter_weights(half_width):
    offsets = np.arange(-half_width, half_width + 1).astype(np.float32)
    bell_curve = np.exp(-offsets * offsets / np.float32(8.0))
    return bell_curve / np.sum(bell_curve)


def taps(targets, length):
    weights = filter_weights(FW)
    table = np.zeros((len(targets), length), np.float32)
    for i, cell in enumerate(targets):
        if cell is not None:
            for k in range(-FW, FW + 1):
                if 0 <= cell + k < length:
                    table[i, cell + k] = weights[k + FW]
    return table


def edge_targets(length):
    gap = [None] * (8 - FW)
    return list(range(-FW, 0)) + gap + list(range(length, length + FW)) + gap


def extended_targets(length):
    gap = [None] * (LANES - FW)
    return list(range(length)) + gap + list(range(-FW, 0)) + list(range(length, length + FW)) + gap


def pick_columns(radial):
    table = np.zeros((16, 2 * radial), np.float32)
    for k in range(FW):
        table[k, k] = 1.0
        table[8 + k, radial - FW + k] = 1.0
    table[FW, radial] = 1.0
    table[8 + FW, 2 * radial - 1] = 1.0
    return table


def halves(x):
    high = x.astype(jnp.bfloat16)
    return high, (x - high.astype(jnp.float32)).astype(jnp.bfloat16)


def product(x, y, dims):
    xh, xl = halves(x) if not isinstance(x, tuple) else x
    yh, yl = halves(y) if not isinstance(y, tuple) else y

    def dot(p, q):
        return lax.dot_general(p, q, (dims, ((), ())), preferred_element_type=jnp.float32)

    both = dot(jnp.concatenate([xh, xl], axis=0), yh)
    count = xh.shape[0]
    return both[:count] + (both[count:] + dot(xh, yl))


PLAIN = ((1,), (0,))
TURNED = ((1,), (1,))


def comparators(count):
    size = 1 << (count - 1).bit_length()
    pairs = []
    p = 1
    while p < size:
        k = p
        while k >= 1:
            for j in range(k % p, size - k, 2 * k):
                for i in range(min(k, size - j - k)):
                    if (i + j) // (2 * p) == (i + j + k) // (2 * p) and i + j + k < count:
                        pairs.append((i + j, i + j + k))
            k //= 2
        p *= 2
    return pairs


def touch_up(count):
    return [
        (i, i + d) for d in (2, 1) for odd in (0, 1) for i in range(count - d) if i // d % 2 == odd
    ]


def sort_rows(tiles, pairs):
    for low, high in pairs:
        swap = tiles[high][-1] < tiles[low][-1]
        first = [jnp.where(swap, y, x) for x, y in zip(tiles[low], tiles[high])]
        second = [jnp.where(swap, x, y) for x, y in zip(tiles[low], tiles[high])]
        tiles[low], tiles[high] = first, second
    return tiles


class Slots:
    def __init__(self, components, cap_tiles, step):
        self.fields = components + 1
        self.cap_tiles, self.step = cap_tiles, step
        self.chunks = cap_tiles // step
        self.chunk_rows = self.fields * step
        self.face = -(-(8 + self.chunks * self.chunk_rows) // 8) * 8
        self.rows = self.face + 8 * components

    def place(self, j):
        return 8 + j * self.chunk_rows


def pack_kernel(
    slots, azim,
    count_hbm, src_hbm, cell_hbm, state_hbm, *refs,
):
    sends_hbm, count_ref, src_ref, cell_ref, face_ref, out_ref, held_ref, in_sems, out_sems = refs
    cap_tiles, step = slots.cap_tiles, slots.step
    components, row_count = src_ref.shape
    fields = components + 1
    tile_count = cell_ref.shape[0]
    radial = face_ref.shape[2]
    seg_count = sends_hbm.shape[0]
    piece = row_count // PIECES
    loads = [
        pltpu.make_async_copy(count_hbm, count_ref, in_sems.at[0]),
        pltpu.make_async_copy(state_hbm.at[:, 0:8, :], face_ref, in_sems.at[1]),
        pltpu.make_async_copy(cell_hbm, cell_ref, in_sems.at[2]),
    ] + [
        pltpu.make_async_copy(
            src_hbm.at[:, k * piece : (k + 1) * piece], src_ref.at[:, k * piece : (k + 1) * piece], in_sems.at[3 + k]
        )
        for k in range(PIECES)
    ]
    for load in loads:
        load.start()
    for load in loads:
        load.wait()
    lane = lax.broadcasted_iota(jnp.int32, (8, LANES), 1)
    sub = lax.broadcasted_iota(jnp.int32, (8, LANES), 0)
    none = float(azim * radial)

    def slot(g, begin):
        count = count_ref[0, g]
        first = begin // LANES
        shift = begin % LANES
        turn = (LANES - shift) % LANES

        def rolled(i):
            t = jnp.minimum(first + i, tile_count - 1)
            src = src_ref[:, pl.ds(pl.multiple_of(t * LANES, LANES), LANES)]
            cell = cell_ref[pl.ds(t, 1), :].astype(jnp.float32)
            both = jnp.concatenate([src, cell, jnp.zeros((8 - fields, LANES), jnp.float32)], axis=0)
            return pltpu.roll(both, turn, 1)

        row = g * slots.rows + slots.face
        for v in range(components):
            for half in range(2):
                out_ref[pl.ds(row + 8 * v + 4 * half, JL), :] = face_ref[
                    v, 0:JL, half * LANES : (half + 1) * LANES
                ]
        head = rolled(0)
        for i in range(cap_tiles):
            tail = rolled(i + 1)
            rows = jnp.where(lane < LANES - shift, head, tail)
            dead = (sub == components) & (lane >= count - i * LANES)
            rows = jnp.where(dead, none, rows)
            held_ref[g // 8, i, pl.ds(g % 8, 8, stride=8), :] = rows
            head = tail
        return begin + count

    lax.fori_loop(0, seg_count, slot, jnp.int32(0))

    def group(h):
        tiles = [
            [held_ref[h, i, 8 * f : 8 * f + 8, :] for f in range(fields)] for i in range(cap_tiles)
        ]
        tiles = sort_rows(tiles, comparators(cap_tiles))
        for again in range(ROUNDS):
            tiles = [[pltpu.roll(x, (37 * i) % LANES, 1) for x in tiles[i]] for i in range(cap_tiles)]
            tiles = sort_rows(tiles, touch_up(cap_tiles))
        bounds = jnp.zeros((8, LANES), jnp.float32)
        for i in range(cap_tiles):
            key = tiles[i][-1]
            least = jnp.min(key, axis=1, keepdims=True)
            most = jnp.max(jnp.where(key < none, key, -1.0), axis=1, keepdims=True)
            bounds = jnp.where(lane == i, jnp.floor(least * (1.0 / radial)), bounds)
            bounds = jnp.where(lane == HALF + i, jnp.floor(most * (1.0 / radial)), bounds)
        row = h * 8 * slots.rows
        out_ref[pl.ds(row, 8, stride=slots.rows), :] = bounds
        for i in range(cap_tiles):
            begin = row + slots.place(i // step) + fields * (i % step)
            for f in range(fields):
                out_ref[pl.ds(begin + f, 8, stride=slots.rows), :] = tiles[i][f]

    stores = []
    for h in range(seg_count // 8):
        group(h)
        for g in range(8 * h, 8 * h + 8):
            store = pltpu.make_async_copy(
                out_ref.at[g * slots.rows : (g + 1) * slots.rows, :], sends_hbm.at[g], out_sems.at[g]
            )
            store.start()
            stores.append(store)
    for store in stores:
        store.wait()


def base_kernel(state_ref, kappa_ref, out_ref, edge_ref):
    components, azim, radial = state_ref.shape
    lane = lax.broadcasted_iota(jnp.int32, (azim, radial), 1)
    sub = lax.broadcasted_iota(jnp.int32, (8, radial), 0)
    first = lane[:1] == 0
    last = lane[:1] == radial - 1
    pick = lax.broadcasted_iota(jnp.int32, (8, radial), 1)
    pick = ((sub == 2) & (pick == 0)) | ((sub == 3) & (pick == radial - 1))
    pick = jnp.where(pick, 1.0, 0.0).astype(jnp.bfloat16)
    none = jnp.zeros((1, radial), jnp.float32)

    def component(v, carry):
        q = state_ref[v]
        both = jnp.concatenate([q[1:], none], axis=0) + jnp.concatenate([none, q[:-1]], axis=0)
        column = both + 4.0 * q
        side = jnp.where(lane == radial - 1, 0.0, pltpu.roll(column, radial - 1, 1)) + jnp.where(
            lane == 0, 0.0, pltpu.roll(column, 1, 1)
        )
        total = side + (4.0 * both - 20.0 * q)
        out_ref[v] = q + (time_step / 6.0) * (kappa_ref[...] * total)

        def along(row):
            right = jnp.where(last, 0.0, pltpu.roll(row, radial - 1, 1))
            left = jnp.where(first, 0.0, pltpu.roll(row, 1, 1))
            return 4.0 * row + right + left

        top, bottom = q[:1], q[-1:]
        high, low = halves(column)
        turned = sum(
            lax.dot_general(pick, x, (TURNED, ((), ())), preferred_element_type=jnp.float32) for x in (high, low)
        )
        edge_ref[v] = jnp.where(
            sub == 0,
            along(top),
            jnp.where(sub == 1, along(bottom), jnp.where(sub == 4, top, jnp.where(sub == 5, bottom, turned))),
        )
        return carry

    lax.fori_loop(0, components, component, 0)


def by_least(slots, live, keys):
    columns = keys.T
    count, rows = keys.shape[0], slots.cap_tiles
    deep = -(-rows // 8) * 8
    length = -(-count * rows // LANES) * LANES
    slot = lax.broadcasted_iota(jnp.int32, keys.shape, 0)
    row = lax.broadcasted_iota(jnp.int32, keys.shape, 1)
    keys = (jnp.where(live, keys, 600.0) * (HALF * count)) + (slot * HALF + row).astype(jnp.float32)
    turned = keys.T
    places = []
    for s in range(count):
        fewer = jnp.zeros((deep, LANES), jnp.float32)
        for other in range(count):
            column = turned[:deep, other : other + 1]
            fewer += jnp.where(column < keys[s : s + 1, :], 1.0, 0.0)
        if deep > rows:
            extra = sum(
                jnp.where(turned[rows:deep, other : other + 1] < keys[s : s + 1, :], 1.0, 0.0)
                for other in range(count)
            )
            places.append(jnp.sum(fewer, axis=0, keepdims=True) - jnp.sum(extra, axis=0, keepdims=True))
        else:
            places.append(jnp.sum(fewer, axis=0, keepdims=True))
    places = jnp.concatenate(places, axis=0).T
    spot = lax.broadcasted_iota(jnp.int32, (deep, length), 1).astype(jnp.float32)
    name = lax.broadcasted_iota(jnp.int32, (deep, length), 0).astype(jnp.float32)
    tables = [jnp.zeros((deep, length), jnp.float32) for k in range(3)]
    for s in range(count):
        here = (places[:deep, s : s + 1] == spot) & (name < rows)
        values = (name + float(s * HALF), columns[:deep, s : s + 1], columns[HALF : HALF + deep, s : s + 1])
        tables = [table + jnp.where(here, value, 0.0) for table, value in zip(tables, values)]
    return [jnp.sum(table, axis=0, keepdims=True) for table in tables]


def by_window(step, count, least, most):
    length = least.shape[1]
    spot = lax.broadcasted_iota(jnp.int32, (1, length), 1)
    far = most
    for q in range(1, step):
        far = jnp.maximum(far, jnp.where(spot + q < count, pltpu.roll(most, length - q, 1), -1.0))
    start = jnp.floor(least * 0.125)
    windows = jnp.floor((far - 8.0 * start) * (1.0 / WINDOW)) + 1.0
    windows = jnp.where((spot % step == 0) & (spot < count), windows, 0.0)
    row = lax.broadcasted_iota(jnp.int32, (length, length), 0)
    earlier = jnp.where(row < lax.broadcasted_iota(jnp.int32, (length, length), 1), 1.0, 0.0).astype(jnp.bfloat16)
    sub = lax.broadcasted_iota(jnp.int32, (8, length), 0)

    def dot(x, y):
        return lax.dot_general(x.astype(jnp.bfloat16), y, (PLAIN, ((), ())), preferred_element_type=jnp.float32)

    before = dot(jnp.where(sub == 0, windows, 0.0), earlier)[:1]
    columns = jnp.where(sub == 0, before, jnp.where(sub == 1, before + windows, 0.0)).T
    items = work_length(length // step)
    item = lax.broadcasted_iota(jnp.int32, (length, items), 1).astype(jnp.float32)
    here = (columns[:, 0:1] <= item) & (item < columns[:, 1:2])
    here = jnp.where(here, 1.0, 0.0).astype(jnp.bfloat16)
    high = jnp.floor(before * (1.0 / 256))
    chunk = (spot // step).astype(jnp.float32)
    found = dot(
        jnp.where(
            sub == 0,
            chunk,
            jnp.where(sub == 1, start, jnp.where(sub == 2, high, jnp.where(sub == 3, before - 256.0 * high, 0.0))),
        ),
        here,
    )
    first = 8.0 * found[1:2] + WINDOW * (item[:1] - (256.0 * found[2:3] + found[3:4]))
    total = jnp.sum(windows).astype(jnp.int32)
    return found[0:1], first, total


def work_length(chunks):
    return -(-(chunks * (256 // WINDOW + 1) + UNROLL) // LANES) * LANES


def add_chunks(slots, own, own_only, meanwhile, got_ref, sum_ref, list_ref, task_ref, order_ref, work_ref, sems):
    seg_count = got_ref.shape[0]
    components, _, radial = sum_ref.shape
    azim = sum_ref.shape[1] - WINDOW
    fields, step = slots.fields, slots.step
    width = step * LANES
    count = -(-seg_count // 8) * 8
    bounds = [got_ref[s, 0:1, :] for s in range(seg_count)]
    if count > seg_count:
        bounds.append(jnp.full((count - seg_count, LANES), -1.0, jnp.float32))
    bounds = jnp.concatenate(bounds, axis=0)
    most = pltpu.roll(bounds, LANES - HALF, 1)
    live = (most >= 0) & (lax.broadcasted_iota(jnp.int32, (count, LANES), 1) < slots.cap_tiles)
    if not own_only:
        live = live & (lax.broadcasted_iota(jnp.int32, (count, LANES), 0) != own)
    total_rows = jnp.sum(jnp.where(live, 1.0, 0.0)).astype(jnp.int32)
    order, least, most = by_least(slots, live, bounds)
    list_ref[0:1, :] = order.astype(jnp.int32)
    chunk, first, total = by_window(step, total_rows, least, most)
    task_ref[0:1, :] = chunk.astype(jnp.int32)
    unroll = OWN_UNROLL if own_only else UNROLL
    task = lax.broadcasted_iota(jnp.int32, first.shape, 1)
    task_ref[1:2, :] = jnp.where(task < total, first.astype(jnp.int32), azim)
    copies = [
        pltpu.make_async_copy(task_ref, work_ref, sems.at[0]),
        pltpu.make_async_copy(list_ref, order_ref, sems.at[1]),
    ]
    for copy in copies:
        copy.start()
    meanwhile()
    cells = lax.broadcasted_iota(jnp.int32, (radial, width), 0).astype(jnp.float32).astype(jnp.bfloat16)
    near = lax.broadcasted_iota(jnp.int32, (WINDOW, width), 0).astype(jnp.float32).astype(jnp.bfloat16)
    lanes = lax.broadcasted_iota(jnp.int32, (1, width), 1)
    none = float(azim * radial)
    for copy in copies:
        copy.wait()

    def block(t):
        c = work_ref[0, t]
        start = pl.multiple_of(work_ref[1, t], 8)
        rows = []
        for q in range(step):
            name = order_ref[0, c * step + q]
            rows.append(got_ref[name // HALF, pl.ds(8 + fields * (name % HALF), fields), :])

        def field(k):
            return jnp.concatenate([x[k : k + 1] for x in rows], axis=1)

        ids = jnp.where(lanes < (total_rows - c * step) * LANES, field(components), none)
        a = jnp.floor(ids * (1.0 / radial))
        b = (ids - radial * a).astype(jnp.bfloat16)
        right = jnp.where(cells == b, jnp.bfloat16(1), jnp.bfloat16(0))
        in_a = near == (a - start.astype(jnp.float32)).astype(jnp.bfloat16)
        highs, lows = [], []
        for v in range(components):
            values = field(v)
            high = values.astype(jnp.bfloat16)
            low = (values - high.astype(jnp.float32)).astype(jnp.bfloat16)
            highs.append(jnp.where(in_a, high, jnp.bfloat16(0)))
            lows.append(jnp.where(in_a, low, jnp.bfloat16(0)))
        left = jnp.concatenate(highs + lows, axis=0)
        part = lax.dot_general(left, right, (TURNED, ((), ())), preferred_element_type=jnp.float32)
        part = part[: components * WINDOW] + part[components * WINDOW :]
        return start, part

    def several(first, size):
        done = [block(first + u) for u in range(size)]
        for start, part in done:
            for v in range(components):
                sum_ref[v, pl.ds(start, WINDOW), :] += part[v * WINDOW : (v + 1) * WINDOW]

    full = (total + unroll - 1 - (0 if own_only else SPARE)) // unroll

    @pl.loop(0, full)
    def _(t):
        several(t * unroll, unroll)

    @pl.loop(0, (jnp.maximum(total - full * unroll, 0) + FEW - 1) // FEW)
    def _(t):
        several(full * unroll + t * FEW, FEW)


def own_kernel(slots, sends_hbm, sum_ref, held_ref, *work):
    own = lax.axis_index("segaz")
    load = pltpu.make_async_copy(sends_hbm.at[own], held_ref.at[0], work[-1])
    load.start()

    def meanwhile():
        sum_ref[...] = jnp.zeros(sum_ref.shape, jnp.float32)

    load.wait()
    add_chunks(slots, own, True, meanwhile, held_ref, sum_ref, *work[:-1])


def rest_kernel(
    slots,
    map_ref, match_ref, got_ref, begun_ref, face_ref, edge_ref, near_ref, far_ref,
    sum_ref, joint_ref, before_ref, after_ref, side_ref,
    *work,
):
    seg_count = got_ref.shape[0]
    components, _, radial = sum_ref.shape
    azim = sum_ref.shape[1] - WINDOW
    own = lax.axis_index("segaz")

    def meanwhile():
        sum_ref[...] = begun_ref[...]
        partner = jnp.int32(0)
        target = match_ref[map_ref[own]]
        for h in range(seg_count):
            partner = jnp.where(map_ref[h] == target, h, partner)
        layer = lax.broadcasted_iota(jnp.int32, (JL, radial), 0)
        strength = jnp.zeros((JL, radial), jnp.float32)
        for l in range(JL):
            strength = jnp.where(layer == l, layer_weights[l], strength)
        for v in range(components):
            tile = got_ref[partner, slots.face + 8 * v : slots.face + 8 * v + 8, :]
            face = jnp.concatenate([tile[:JL], tile[JL:]], axis=1)
            joint_ref[v, 0:JL, :] = strength * (face - face_ref[v, 0:JL, :])
            joint_ref[v, JL:8, :] = jnp.zeros((8 - JL, radial), jnp.float32)

    add_chunks(slots, own, False, meanwhile, got_ref, sum_ref, *work)

    near = halves(near_ref[...])
    far = halves(far_ref[...])
    inner = tuple(x[:, :radial] for x in far)
    ends = tuple(jnp.concatenate([x[:, :16], x[:, azim - 16 :]], axis=1) for x in near)
    rows, columns = [], []
    for v in range(components):
        cells_v = halves(sum_ref[v, 0:azim, :])
        edges = tuple(jnp.concatenate([x[:16], x[azim - 16 :]], axis=0) for x in cells_v)
        rows.append(product(ends, edges, PLAIN))
        columns.append(product(near, cells_v, TURNED))
    rows = product(jnp.concatenate(rows, axis=0), inner, PLAIN)
    columns = product(jnp.concatenate(columns, axis=0), far, PLAIN)
    sub = lax.broadcasted_iota(jnp.int32, (8, LANES), 0)
    lane = lax.broadcasted_iota(jnp.int32, (8, LANES), 1)
    half = LANES
    for v in range(components):
        row = rows[16 * v : 16 * v + 16]
        column = columns[16 * v : 16 * v + 16]
        edge = edge_ref[v]
        wide = lax.broadcasted_iota(jnp.int32, (8, radial), 0)
        after_ref[v, :, :radial] = jnp.where(wide == FW, edge[1:2], row[8:16])
        before_ref[v, :, :radial] = jnp.where(
            wide == FW - 1, edge[0:1], jnp.concatenate([row[FW:8], row[0:FW]], axis=0)
        )
        bottom, top = edge[5:6], edge[4:5]
        left_corner = jnp.where(lane[:1] == 0, bottom[:, :half], 0.0)
        right_corner = jnp.where(lane[:1] == 0, pltpu.roll(bottom[:, radial - half :], 1, 1), 0.0)
        after_ref[v, :, radial : radial + half] = jnp.where(
            sub == FW, left_corner, column[0:8, radial + half : radial + 2 * half]
        )
        after_ref[v, :, radial + half : radial + 2 * half] = jnp.where(
            sub == FW, right_corner, column[8:16, radial + half : radial + 2 * half]
        )
        left_corner = jnp.where(lane[:1] == half - 1, pltpu.roll(top[:, :half], half - 1, 1), 0.0)
        right_corner = jnp.where(lane[:1] == half - 1, top[:, radial - half :], 0.0)
        before_ref[v, :, radial : radial + half] = jnp.where(
            sub == FW, left_corner, column[0:8, radial : radial + half]
        )
        before_ref[v, :, radial + half : radial + 2 * half] = jnp.where(
            sub == FW, right_corner, column[8:16, radial : radial + half]
        )
        side_ref[v, 0:8, :] = jnp.where(wide == FW, edge[2:3], column[0:8, :radial])
        side_ref[v, 8:16, :] = jnp.where(wide == FW, edge[3:4], column[8:16, :radial])


def inner_kernel(sum_ref, base_ref, joint_ref, band_ref, out_ref):
    components, azim, radial = base_ref.shape
    band = halves(band_ref[...])

    def component(v, carry):
        across = product(sum_ref[v, 0:azim, :], band, PLAIN)
        both = product(band, across, PLAIN)
        out_ref[v] = base_ref[v] + time_step * both
        out_ref[v, 0:8, :] += time_step * joint_ref[v]
        return carry

    lax.fori_loop(0, components, component, 0)


def corner_kernel(side_ref, prior_ref, next_ref, left_ref, right_ref):
    radial = left_ref.shape[2]
    for out_ref, begin, corner in ((left_ref, 0, radial), (right_ref, 8, radial + LANES)):
        out_ref[:, :, :LANES] = (
            side_ref[:, begin : begin + 8, :LANES] + prior_ref[:, :, corner : corner + LANES]
        )
        out_ref[:, :, LANES:] = (
            side_ref[:, begin : begin + 8, LANES:] + next_ref[:, :, corner : corner + LANES]
        )


def final_kernel(inner_ref, kappa_ref, prior_ref, next_ref, left_ref, right_ref, pick_ref, out_hbm, out_ref, sems):
    components, azim, radial = out_ref.shape
    pick = pick_ref[...].astype(jnp.bfloat16)
    sub = lax.broadcasted_iota(jnp.int32, (8, radial), 0)
    stores = []
    for v in range(components):
        parts = halves(jnp.concatenate([left_ref[v], right_ref[v]], axis=0))
        sides = sum(
            lax.dot_general(x, pick, (((0,), (0,)), ((), ())), preferred_element_type=jnp.float32) for x in parts
        )
        kappa = kappa_ref[...]
        total = inner_ref[v] + time_step * sides[:, :radial] + (time_step / 6.0) * (kappa * sides[:, radial:])
        prior = prior_ref[v, :, :radial]
        add = jnp.where(sub < FW, prior, 0.0) + jnp.where(
            sub == 0, kappa[0:8] * (prior[FW : FW + 1] * (1.0 / 6.0)), 0.0
        )
        out_ref[v, 0:8, :] = total[0:8] + time_step * add
        out_ref[v, 8 : azim - 8, :] = total[8 : azim - 8]
        nxt = next_ref[v, :, :radial]
        add = jnp.where(sub >= 8 - FW, nxt, 0.0) + jnp.where(
            sub == 7, kappa[azim - 8 : azim] * (nxt[FW - 1 : FW] * (1.0 / 6.0)), 0.0
        )
        out_ref[v, azim - 8 : azim, :] = total[azim - 8 : azim] + time_step * add
        store = pltpu.make_async_copy(out_ref.at[v], out_hbm.at[v], sems.at[v])
        store.start()
        stores.append(store)
    for store in stores:
        store.wait()


def call(kernel, outs, ins, scratch=(), cost=None, to="vmem", room=48):
    spaces = {"smem": pltpu.SMEM, "vmem": pltpu.VMEM, "hbm": pltpu.HBM, "any": pl.ANY}

    def spec(where):
        if isinstance(where, str):
            return pl.BlockSpec(memory_space=spaces[where])
        return pl.BlockSpec(where, lambda i: (0,) * len(where))

    return pl.pallas_call(
        kernel,
        grid=(1,),
        out_shape=[jax.ShapeDtypeStruct(shape, jnp.float32) for shape in outs],
        in_specs=[spec(where) for where in ins],
        out_specs=[spec(to)] * len(outs),
        scratch_shapes=list(scratch),
        cost_estimate=None
        if cost is None
        else pl.CostEstimate(flops=cost, bytes_accessed=cost // 1000, transcendentals=0),
        compiler_params=pltpu.CompilerParams(vmem_limit_bytes=room << 20),
    )


def shifted(strip, axis, way):
    count = lax.axis_size(axis)
    pairs = [(i, i + 1) if way > 0 else (i + 1, i) for i in range(count - 1)]
    return lax.ppermute(strip, axis, pairs)


def local(state, kappa, drop_src, drop_cell, drop_count, part_map, match_block):
    components, azim, radial = state.shape
    row_count = drop_src.shape[1]
    seg_count = lax.axis_size("segaz")
    capacity = 5 * row_count // (4 * seg_count)
    cap_tiles = capacity // LANES
    slots = Slots(components, cap_tiles, STEP if cap_tiles % STEP == 0 else 2)
    face = (components, 8, radial)
    whole = state.shape
    sums = (components, azim + WINDOW, radial)
    strip = (components, 8, 2 * radial)
    sides = (components, 8, radial)
    (sends,) = call(
        functools.partial(pack_kernel, slots, azim),
        [(seg_count, slots.rows, LANES)],
        ["hbm"] * 4,
        [
            pltpu.SMEM(drop_count.shape[:1] + (seg_count,), jnp.int32),
            pltpu.VMEM(drop_src.shape, jnp.float32),
            pltpu.VMEM((row_count // LANES, LANES), jnp.int32),
            pltpu.VMEM(face, jnp.float32),
            pltpu.VMEM((seg_count * slots.rows, LANES), jnp.float32),
            pltpu.VMEM((seg_count // 8, cap_tiles, 64, LANES), jnp.float32),
            pltpu.SemaphoreType.DMA((3 + PIECES,)),
            pltpu.SemaphoreType.DMA((seg_count,)),
        ],
        to="hbm",
        room=62,
    )(drop_count, drop_src, drop_cell.reshape(-1, LANES), state)
    got = lax.all_to_all(sends, "segaz", split_axis=0, concat_axis=0, tiled=True)

    def work(count):
        length = -(-(-(-count // 8) * 8) * cap_tiles // LANES) * LANES
        return [
            pltpu.VMEM((8, length), jnp.int32),
            pltpu.VMEM((8, work_length(length // slots.step)), jnp.int32),
            pltpu.SMEM((8, length), jnp.int32),
            pltpu.SMEM((8, work_length(length // slots.step)), jnp.int32),
            pltpu.SemaphoreType.DMA((2,)),
        ]

    (begun,) = call(
        functools.partial(own_kernel, slots),
        [sums],
        ["hbm"],
        [pltpu.VMEM((1, slots.rows, LANES), jnp.float32)] + work(1) + [pltpu.SemaphoreType.DMA(())],
        cost=1 << 23,
    )(sends)
    still, edge = call(base_kernel, [whole, face], ["vmem", "vmem"], cost=1 << 22)(state, kappa)
    near = jnp.asarray(taps(edge_targets(azim), azim))
    far = jnp.asarray(taps(extended_targets(azim), azim).T)
    band = jnp.asarray(taps(list(range(azim)), azim))
    source, joint, before, after, side = call(
        functools.partial(rest_kernel, slots),
        [sums, face, strip, strip, (components, 16, radial)],
        ["smem", "smem", "vmem", "vmem", face, "vmem", "vmem", "vmem"],
        work(seg_count),
    )(part_map, match_block, got, begun, state, edge, near, far)
    prior = shifted(after, "segaz", 1)
    nxt = shifted(before, "segaz", -1)
    (inner,) = call(inner_kernel, [whole], ["vmem"] * 4, cost=1 << 22)(source, still, joint, band)
    to_left, to_right = call(corner_kernel, [sides, sides], ["vmem"] * 3)(side, prior, nxt)
    left = shifted(to_right, "rad", 1)
    right = shifted(to_left, "rad", -1)
    pick = jnp.asarray(pick_columns(radial))
    (result,) = call(
        final_kernel,
        [whole],
        ["vmem"] * 7,
        [pltpu.VMEM(whole, jnp.float32), pltpu.SemaphoreType.DMA((components,))],
        to="hbm",
    )(inner, kappa, prior, nxt, left, right, pick)
    return result


def solution(mesh):
    return jax.shard_map(
        local,
        mesh=mesh,
        in_specs=(
            P(None, "segaz", "rad"),
            P("segaz", "rad"),
            P(None, ("segaz", "rad")),
            P(("segaz", "rad")),
            P(("segaz", "rad"), None),
            P(),
            P(),
        ),
        out_specs=P(None, "segaz", "rad"),
        check_vma=False,
    )
```
